32 devices in a mesh: parts: 2 (over y), tensor: 4 (over z), dp: 4 (over x, core).
Axes of the slice: x: 2, y: 2, z: 4, core: 2. Of those that a mesh axis runs over, the one named last changes fastest.
Arguments:
- activations: bfloat16 [64, 120, 8192], P(('parts', 'dp'), None, 'tensor'), parts along dimension 0, may hold values from -6 to 6
- frozen_weight: bfloat16 [8192, 2048], P('tensor'), may hold values from -0.09375 to 0.09375
- cotangent: bfloat16 [64, 120, 2048], P(('parts', 'dp'), None, 'tensor'), parts along dimension 0, may hold values from -6 to 6
- adapter_down_weight: bfloat16 [256, 16, 8192], P(('parts', 'dp'), None, 'tensor'), parts along dimension 0, may hold values from -0.0625 to 0.0625
- adapter_up_weight: bfloat16 [256, 16, 2048], P(('parts', 'dp'), None, 'tensor'), parts along dimension 0, may hold values from -1.5 to 1.5
- sequence_adapter: int32 [64], P('parts'), parts along dimension 0, may hold values from 0 to 127, as said below
- adapter_store_row: int32 [256], P('parts'), parts along dimension 0, may hold values from 0 to 127, as said below
- group_live_counts: int32 [8], P(('parts', 'dp')), parts along dimension 0, may hold values from 1 to 8, as said below
Outputs:
- key_value_output: bfloat16 [64, 120, 2048], P(('parts', 'dp'), None, 'tensor'), parts along dimension 0
- grad_input: bfloat16 [64, 120, 8192], P(('parts', 'dp'), None, 'tensor'), parts along dimension 0
- grad_down: float32 [256, 16, 8192], P(('parts', 'dp'), None, 'tensor'), parts along dimension 0
- grad_up: float32 [256, 16, 2048], P(('parts', 'dp'), None, 'tensor'), parts along dimension 0
The draws below stay inside these ranges and needn't reach their ends.
There are 2 independent parts, one for each index of `parts`. The reference program is written for one: setup_inputs(seed, part) draws one part's arguments, and reference() takes and returns one part's arrays. A program takes and returns all parts, laid end to end along the dimension named above; an argument that names none is the same for every part. Nothing has to cross between parts.
Inputs may be any that keep to these rules, and one draw needn't show every extreme that they name: `adapter_store_row`: A permutation: each store row holds one adapter. Store rows g * 32 to (g + 1) * 32 - 1 lie on index g of dp. `sequence_adapter`: among the 8 slots of one data group, at most 2 use adapters whose store rows lie on one index of dp, and every group reaches 2 for some index. Slots may share an adapter. `group_live_counts`: live slots of a group come first. Some group is full and some group has one live sequence.
All inputs are finite; a program needn't handle non-finite values.
Results may differ from the reference program's by a relative error of at most 0.013.
Values may be sent and summed in bfloat16 or wider, within the bound.
A program may use at most 128 MiB of HBM per device.

```python
import jax
import jax.numpy as jnp
from jax import lax

MODEL_WIDTH = 8192
KEY_VALUE_WIDTH = 2048
ADAPTER_RANK = 16
OWN_DEV = 32
SEQ_CAP = 8
SEQUENCE_LENGTH = 120
SEQUENCE_SLOTS = 32
ADAPTER_COUNT = 128
N_TENSOR = 4


def shared_home(key):
    return jax.random.permutation(key, ADAPTER_COUNT).astype(jnp.int32)


def draw_adapter_store_row(key, part):
    return shared_home(key)


def draw_sequence_adapter(key, part):
    home_rows = shared_home(key)
    key = jax.random.fold_in(key, 3)
    group_count = SEQUENCE_SLOTS // SEQ_CAP
    inverse = jnp.argsort(home_rows).astype(jnp.int32)
    keys = jax.random.split(key, 4)
    item_count = 2 * group_count
    item_ids = jnp.arange(item_count, dtype=jnp.int32)
    top_owner = home_rows[ADAPTER_COUNT - 1] // OWN_DEV
    bottom_owner = home_rows[0] // OWN_DEV
    forced = jax.random.randint(keys[0], (group_count,), 0, group_count).astype(jnp.int32)
    forced = forced.at[0].set(top_owner).at[1].set(bottom_owner)
    local_items = jax.random.randint(keys[1], (group_count, item_count), 0, OWN_DEV).astype(jnp.int32)
    local_items = local_items.at[0, top_owner].set(home_rows[ADAPTER_COUNT - 1] % OWN_DEV)
    local_items = local_items.at[1, bottom_owner].set(home_rows[0] % OWN_DEV)
    scores = jax.random.randint(keys[2], (group_count, item_count), 0, 1 << 20).astype(jnp.int32) * item_count + item_ids[None, :]
    is_forced = item_ids[None, :] % group_count == forced[:, None]
    scores = jnp.where(is_forced, scores + (1 << 28), scores)
    chosen = jnp.argsort(-scores, axis=1)[:, :SEQ_CAP].astype(jnp.int32)
    shuffle = jax.random.randint(keys[3], (group_count, SEQ_CAP), 0, 1 << 20).astype(jnp.int32) * SEQ_CAP + jnp.arange(SEQ_CAP, dtype=jnp.int32)[None, :]
    order = jnp.argsort(shuffle, axis=1).astype(jnp.int32)
    chosen = jnp.take_along_axis(chosen, order, axis=1)
    owners = chosen % group_count
    picked = jnp.take_along_axis(local_items, chosen, axis=1)
    return inverse[owners * OWN_DEV + picked].reshape(SEQUENCE_SLOTS).astype(jnp.int32)


def draw_group_live_counts(key, part):
    key = jax.random.fold_in(key, 5)
    group_count = SEQUENCE_SLOTS // SEQ_CAP
    keys = jax.random.split(key, 3)
    counts = jax.random.randint(keys[0], (group_count,), 1, SEQ_CAP + 1).astype(jnp.int32)
    full_group = jax.random.randint(keys[1], (), 0, group_count).astype(jnp.int32)
    single = (full_group + 1 + jax.random.randint(keys[2], (), 0, group_count - 1).astype(jnp.int32)) % group_count
    group_ids = jnp.arange(group_count, dtype=jnp.int32)
    counts = jnp.where(group_ids == full_group, SEQ_CAP, jnp.where(group_ids == single, 1, counts))
    return counts.astype(jnp.int32)


def spiked(values, stream_key, source, target, parts, factor):
    def block_of(axis_at):
        return (jnp.arange(values.shape[axis_at]) // (values.shape[axis_at] // parts)).reshape((-1,) + (1,) * (values.ndim - 1 - axis_at))

    near = jax.random.permutation(stream_key, parts)[block_of(target)]
    other_side = (block_of(target) + parts // 2) % parts
    return jnp.where((block_of(source) == near) | (block_of(source) == other_side), factor * values, values)


def shard_levels(key, extent, shards, smallest, top_value):
    def one(axis_at, blocks):
        steps = jax.random.uniform(jax.random.fold_in(jax.random.fold_in(key, 6), axis_at), (blocks,), jnp.float32, smallest / len(shards), top_value / len(shards))
        return jnp.repeat(jnp.exp(steps), extent[axis_at] // blocks).reshape((-1,) + (1,) * (len(extent) - axis_at - 1))

    factor_of = one(*shards[0])
    for cut in shards[1:]:
        factor_of = factor_of * one(*cut)
    return factor_of


def gaussian(key, extent, width, limit, cuts=(), kind=jnp.bfloat16):
    loudness = shard_levels(key, extent, cuts, -0.22, 0.18) if cuts else 1.0
    values = jax.random.normal(key, extent, jnp.float32) * width * loudness
    return jnp.minimum(jnp.maximum(values, -limit), limit).astype(kind)


def heavy_noise(own_key, dims, scale, limit, shards, heavy, held_as=jnp.bfloat16):
    array = scale * jax.random.normal(own_key, dims, jnp.float32)
    if shards:
        array = array * shard_levels(own_key, dims, shards, -0.22, 0.18)
    return jnp.clip(spiked(array, jax.random.fold_in(own_key, 3), *heavy), -limit, limit).astype(held_as)


def setup_inputs(seed: int = 0, part: int = 0) -> dict:
    key_of = jax.random.split(jax.random.key(seed), 9)
    part_keys = jax.random.split(jax.random.fold_in(key_of[8], part), 9)
    activations = gaussian(part_keys[0], (SEQUENCE_SLOTS, SEQUENCE_LENGTH, MODEL_WIDTH), 1.0, 6.0, ((0, 4), (2, 4)))
    frozen_weight = heavy_noise(key_of[1], (MODEL_WIDTH, KEY_VALUE_WIDTH), MODEL_WIDTH ** -0.5, 0.09375, ((0, 4),), (0, 1, 4, 2.0))
    cotangent = gaussian(part_keys[2], (SEQUENCE_SLOTS, SEQUENCE_LENGTH, KEY_VALUE_WIDTH), 1.0, 6.0, ((0, 4), (2, 4)))
    adapter_down_weight = gaussian(part_keys[3], (ADAPTER_COUNT, ADAPTER_RANK, MODEL_WIDTH), MODEL_WIDTH ** -0.5, 0.0625, ((0, 4), (2, 4)))
    adapter_up_weight = gaussian(part_keys[4], (ADAPTER_COUNT, ADAPTER_RANK, KEY_VALUE_WIDTH), ADAPTER_RANK ** -0.5, 1.5, ((0, 4), (2, 4)))
    sequence_adapter = draw_sequence_adapter(jax.random.fold_in(jax.random.fold_in(key_of[8], part), 71), part)
    adapter_store_row = draw_adapter_store_row(jax.random.fold_in(jax.random.fold_in(key_of[8], part), 71), part)
    group_live_counts = draw_group_live_counts(jax.random.fold_in(jax.random.fold_in(key_of[8], part), 71), part)
    return {"activations": activations, "frozen_weight": frozen_weight, "cotangent": cotangent, "adapter_down_weight": adapter_down_weight, "adapter_up_weight": adapter_up_weight, "sequence_adapter": sequence_adapter, "adapter_store_row": adapter_store_row, "group_live_counts": group_live_counts}


adapter_scale = 2.0


def reference(activations, frozen_weight, cotangent, adapter_down_weight, adapter_up_weight, sequence_adapter, adapter_store_row, group_live_counts):
    seq_index = jnp.arange(SEQUENCE_SLOTS, dtype=jnp.int32)
    live_sequence_mask = ((seq_index % SEQ_CAP) < group_live_counts[seq_index // SEQ_CAP]).astype(jnp.float32)[:, None, None]
    adapter_rows = adapter_store_row[sequence_adapter]
    down_weight_slice = adapter_down_weight[adapter_rows].astype(jnp.float32)
    up_weight_slice = adapter_up_weight[adapter_rows].astype(jnp.float32)
    input_tokens = activations.astype(jnp.float32)
    reduced_rank_rows = jnp.einsum('cfy,cjy->cfj', input_tokens, down_weight_slice).astype(jnp.bfloat16)
    block_width = MODEL_WIDTH // N_TENSOR
    flat_rows = activations.reshape(SEQUENCE_SLOTS * SEQUENCE_LENGTH, MODEL_WIDTH)

    def add_block(running, block_index):
        piece_rows = lax.dynamic_slice_in_dim(flat_rows, block_index * block_width, block_width, 1)
        weight_rows = lax.dynamic_slice_in_dim(frozen_weight, block_index * block_width, block_width, 0)
        block_term = jnp.dot(piece_rows, weight_rows, preferred_element_type=jnp.float32).astype(jnp.bfloat16)
        block_term = lax.optimization_barrier(block_term).astype(jnp.float32)
        return running + block_term, None

    frozen_total, _ = lax.scan(add_block, jnp.zeros((SEQUENCE_SLOTS * SEQUENCE_LENGTH, KEY_VALUE_WIDTH), jnp.float32), jnp.arange(N_TENSOR, dtype=jnp.int32))
    frozen_total = frozen_total.reshape(SEQUENCE_SLOTS, SEQUENCE_LENGTH, KEY_VALUE_WIDTH)
    adapter_contribution = jnp.einsum('slr,sro->slo', reduced_rank_rows.astype(jnp.float32), up_weight_slice)
    key_value_output = ((frozen_total + adapter_scale * adapter_contribution) * live_sequence_mask).astype(jnp.bfloat16)
    masked = cotangent * live_sequence_mask.astype(jnp.bfloat16)
    masked_float = masked.astype(jnp.float32)
    backward_rank_rows = (adapter_scale * jnp.einsum('bvg,bqg->bvq', masked_float, up_weight_slice)).astype(jnp.bfloat16)
    backward_float = backward_rank_rows.astype(jnp.float32)
    frozen_path = lax.dot_general(masked.reshape(SEQUENCE_SLOTS * SEQUENCE_LENGTH, KEY_VALUE_WIDTH), frozen_weight, (((1,), (1,)), ((), ())), preferred_element_type=jnp.float32)
    input_gradient = frozen_path.reshape(SEQUENCE_SLOTS, SEQUENCE_LENGTH, MODEL_WIDTH) + jnp.einsum('qip,qpb->qib', backward_float, down_weight_slice)
    grad_input = (input_gradient * live_sequence_mask).astype(jnp.bfloat16)
    down_contributions = jnp.einsum('ihn,ihx->inx', backward_float, input_tokens)
    up_contributions = adapter_scale * jnp.einsum('tun,tuq->tnq', reduced_rank_rows.astype(jnp.float32), masked_float)
    grad_down = jax.ops.segment_sum(down_contributions, adapter_rows, ADAPTER_COUNT)
    grad_up = jax.ops.segment_sum(up_contributions, adapter_rows, ADAPTER_COUNT)
    return key_value_output, grad_input, grad_down, grad_up
```

```python
import functools

import jax
import jax.numpy as jnp
from jax import lax
from jax.experimental import pallas as pl
from jax.experimental.pallas import tpu as pltpu
from jax.sharding import PartitionSpec as P

CAP_OWN = 2


adapter_scale = 2.0


CHUNKS = 4
MESH = pl.DeviceIdType.MESH
NT = (((1,), (1,)), ((), ()))
TN = (((0,), (0,)), ((), ()))


def line_kernel(
    n, chunks, slots,
    x_hbm, w_hbm, cot_ref, alive_ref, down_ref, up_ref,
    kv_ref, gin_ref, gdown_ref, gup_ref,
    x_ref, w_ref, full, part, from_left, from_right, acc, small, lowt, backt,
    load_sem, ag_recv, ag_right, ag_left, rs_recv_r, rs_recv_l, rs_send_r, rs_send_l,
    small_send, small_recv,
):
    me = lax.axis_index("tensor")
    rows, width = cot_ref.shape
    depth = x_ref.shape[1]
    rank = small.shape[1] // 2
    size = rows // chunks
    length = rows // slots
    last = n - 1
    mirror = last - me

    def chunk(c):
        return pl.ds(pl.multiple_of(c * size, size), size)

    def columns(d):
        return pl.ds(pl.multiple_of(d * width, width), width)

    def ag_copy(b, c, to_right):
        return pltpu.make_async_remote_copy(
            src_ref=full.at[b, chunk(c)],
            dst_ref=full.at[b, chunk(c)],
            send_sem=(ag_right if to_right else ag_left).at[b, c],
            recv_sem=ag_recv.at[b, c],
            device_id={"tensor": me + 1 if to_right else me - 1},
            device_id_type=MESH,
        )

    def rs_copy(d, c, to_right):
        return pltpu.make_async_remote_copy(
            src_ref=part.at[d, chunk(c)],
            dst_ref=(from_left if to_right else from_right).at[d, chunk(c)],
            send_sem=(rs_send_r if to_right else rs_send_l).at[d, c],
            recv_sem=(rs_recv_r if to_right else rs_recv_l).at[d, c],
            device_id={"tensor": me + 1 if to_right else me - 1},
            device_id_type=MESH,
        )

    def small_copy(peer, slot):
        return pltpu.make_async_remote_copy(
            src_ref=small.at[slot],
            dst_ref=small.at[slot],
            send_sem=small_send.at[peer],
            recv_sem=small_recv.at[slot],
            device_id={"tensor": peer},
            device_id_type=MESH,
        )

    load_x = pltpu.make_async_copy(x_hbm, x_ref, load_sem.at[0])
    load_w = pltpu.make_async_copy(w_hbm, w_ref, load_sem.at[1])
    load_x.start()
    load_w.start()
    barrier = pltpu.get_barrier_semaphore()
    for step in range(1, n):
        pl.semaphore_signal(
            barrier, inc=1, device_id={"tensor": lax.rem(me + step, n)}, device_id_type=MESH
        )
    full[me] = (cot_ref[...].astype(jnp.float32) * alive_ref[...]).astype(full.dtype)
    pl.semaphore_wait(barrier, n - 1)

    @pl.loop(0, chunks)
    def _(c):
        @pl.when(me < last)
        def _():
            ag_copy(me, c, True).start()

        @pl.when(me > 0)
        def _():
            ag_copy(me, c, False).start()

    shape = (slots * rank, rows)
    slot_of_row = lax.broadcasted_iota(jnp.int32, shape, 0) // rank
    slot_of_column = lax.broadcasted_iota(jnp.int32, shape, 1) // length
    diagonal = slot_of_row == slot_of_column

    def compact(wide):
        wide = jnp.where(diagonal, wide, 0.0)
        total = wide[0:rank]
        for s in range(1, slots):
            total = total + wide[s * rank : (s + 1) * rank]
        return total

    back_part = compact(
        lax.dot_general(up_ref[...], full[me], NT, preferred_element_type=jnp.float32)
    )
    small[me, rank:, :] = (adapter_scale * back_part).astype(small.dtype)
    load_x.wait()
    low_part = compact(
        lax.dot_general(down_ref[...], x_ref[...], NT, preferred_element_type=jnp.float32)
    )
    small[me, :rank, :] = low_part.astype(small.dtype)
    for step in range(1, n):
        small_copy(lax.rem(me + step, n), me).start()
    load_w.wait()

    @pl.loop(0, n)
    def _(k):
        d = jnp.where(me == 0, last - k, k)

        @pl.loop(0, chunks)
        def _(c):
            part[d, chunk(c), :] = jnp.dot(
                x_ref[chunk(c), :], w_ref[:, columns(d)], preferred_element_type=jnp.float32
            ).astype(part.dtype)

            @pl.when((me == 0) & (d > 0))
            def _():
                rs_copy(d, c, True).start()

            @pl.when((me == last) & (d < last))
            def _():
                rs_copy(d, c, False).start()

    def frozen(b, first):
        @pl.loop(0, chunks)
        def _(c):
            @pl.loop(0, depth // width)
            def _(j):
                piece = lax.dot_general(
                    full[b, chunk(c), :],
                    w_ref[columns(j), columns(b)],
                    NT,
                    preferred_element_type=jnp.float32,
                )
                if first:
                    acc[chunk(c), columns(j)] = piece
                else:
                    acc[chunk(c), columns(j)] += piece

    frozen(me, True)

    def receive(q, c):
        @pl.when(q < me)
        def _():
            b = me - 1 - q
            ag_copy(b, c, True).wait_recv()

            @pl.when(me < last)
            def _():
                ag_copy(b, c, True).start()

        @pl.when((q >= me) & (me > 0))
        def _():
            d = last - (q - me)
            rs_copy(d, c, True).wait_recv()
            part[d, chunk(c), :] = (
                part[d, chunk(c), :].astype(jnp.float32)
                + from_left[d, chunk(c), :].astype(jnp.float32)
            ).astype(part.dtype)
            rs_copy(d, c, True).start()

        @pl.when(q < mirror)
        def _():
            b = me + 1 + q
            ag_copy(b, c, False).wait_recv()

            @pl.when(me > 0)
            def _():
                ag_copy(b, c, False).start()

        @pl.when((q >= mirror) & (me < last))
        def _():
            d = q - mirror
            rs_copy(d, c, False).wait_recv()
            part[d, chunk(c), :] = (
                part[d, chunk(c), :].astype(jnp.float32)
                + from_right[d, chunk(c), :].astype(jnp.float32)
            ).astype(part.dtype)
            rs_copy(d, c, False).start()

    @pl.loop(0, last)
    def _(q):
        @pl.loop(0, chunks)
        def _(c):
            receive(q, c)

        @pl.when(q < me)
        def _():
            frozen(me - 1 - q, False)

        @pl.when(q < mirror)
        def _():
            frozen(me + 1 + q, False)

    for step in range(1, n):
        source = lax.rem(me + step, n)
        small_copy(source, source).wait_recv()
    total = small[0].astype(jnp.float32)
    for b in range(1, n):
        total = total + small[b].astype(jnp.float32)
    low = jnp.where(diagonal, jnp.concatenate([total[:rank]] * slots, axis=0), 0.0)
    back = jnp.where(diagonal, jnp.concatenate([total[rank:]] * slots, axis=0), 0.0)
    lowt[...] = low.astype(lowt.dtype)
    backt[...] = back.astype(backt.dtype)
    gup_ref[...] = (
        adapter_scale
        * jnp.dot(lowt[...], full[me], preferred_element_type=jnp.float32)
    ).astype(gup_ref.dtype)

    @pl.loop(0, depth // width)
    def _(j):
        gdown_ref[:, columns(j)] = jnp.dot(
            backt[...], x_ref[:, columns(j)], preferred_element_type=jnp.float32
        ).astype(gdown_ref.dtype)
        gin_ref[:, columns(j)] = (
            alive_ref[...]
            * (
                acc[:, columns(j)]
                + lax.dot_general(
                    backt[...], down_ref[:, columns(j)], TN, preferred_element_type=jnp.float32
                )
            )
        ).astype(gin_ref.dtype)

    acc[:, :width] = adapter_scale * lax.dot_general(
        lowt[...], up_ref[...], TN, preferred_element_type=jnp.float32
    )

    def rs_finish(c, to_right):
        rs_copy(me, c, to_right).wait_recv()
        arrived = from_left if to_right else from_right
        acc[chunk(c), :width] += arrived[me, chunk(c), :].astype(jnp.float32)

    @pl.loop(0, chunks)
    def _(c):
        acc[chunk(c), :width] += part[me, chunk(c), :].astype(jnp.float32)

        @pl.when(me > 0)
        def _():
            rs_finish(c, True)

        @pl.when(me < last)
        def _():
            rs_finish(c, False)

        kv_ref[chunk(c), :] = (alive_ref[chunk(c), :] * acc[chunk(c), :width]).astype(kv_ref.dtype)

    def drain(b, c):
        @pl.when((b <= me) & (me < last))
        def _():
            ag_copy(b, c, True).wait_send()

        @pl.when((b >= me) & (me > 0))
        def _():
            ag_copy(b, c, False).wait_send()

        @pl.when(b > me)
        def _():
            rs_copy(b, c, True).wait_send()

        @pl.when(b < me)
        def _():
            rs_copy(b, c, False).wait_send()

    for step in range(1, n):
        small_copy(lax.rem(me + step, n), me).wait_send()

    @pl.loop(0, n)
    def _(b):
        @pl.loop(0, chunks)
        def _(c):
            drain(b, c)


def line_call(n, slots, x, w, cot, alive, down, up):
    rows, depth = x.shape
    width = cot.shape[1]
    panel = down.shape[0]
    rank = panel // slots
    bf16 = jnp.bfloat16
    vmem = pl.BlockSpec(memory_space=pltpu.VMEM)
    hbm = pl.BlockSpec(memory_space=pl.ANY)
    dma = pltpu.SemaphoreType.DMA((n, CHUNKS))
    return pl.pallas_call(
        functools.partial(line_kernel, n, CHUNKS, slots),
        out_shape=(
            jax.ShapeDtypeStruct((rows, width), bf16),
            jax.ShapeDtypeStruct((rows, depth), bf16),
            jax.ShapeDtypeStruct((panel, depth), bf16),
            jax.ShapeDtypeStruct((panel, width), bf16),
        ),
        in_specs=[hbm, hbm, vmem, vmem, vmem, vmem],
        out_specs=(vmem, vmem, vmem, vmem),
        scratch_shapes=[
            pltpu.VMEM((rows, depth), bf16),
            pltpu.VMEM(w.shape, bf16),
            pltpu.VMEM((n, rows, width), bf16),
            pltpu.VMEM((n, rows, width), bf16),
            pltpu.VMEM((n, rows, width), bf16),
            pltpu.VMEM((n, rows, width), bf16),
            pltpu.VMEM((rows, depth), jnp.float32),
            pltpu.VMEM((n, 2 * rank, rows), bf16),
            pltpu.VMEM((panel, rows), bf16),
            pltpu.VMEM((panel, rows), bf16),
            pltpu.SemaphoreType.DMA((2,)),
            dma, dma, dma, dma, dma, dma, dma,
            pltpu.SemaphoreType.DMA((n,)),
            pltpu.SemaphoreType.DMA((n,)),
        ],
        compiler_params=pltpu.CompilerParams(
            collective_id=0, has_side_effects=True, vmem_limit_bytes=56 << 20
        ),
        cost_estimate=pl.CostEstimate(
            flops=4 * rows * depth * n * width, bytes_accessed=30_000_000, transcendentals=0
        ),
    )(x, w, cot, alive, down, up)


def shards(
    activations,
    frozen_weight,
    cotangent,
    adapter_down_weight,
    adapter_up_weight,
    sequence_adapter,
    adapter_store_row,
    group_live_counts,
):
    group_total = lax.axis_size("dp")
    slot_count, seq_length, dim_shard = activations.shape
    holder_count = adapter_down_weight.shape[0]
    output_portion = adapter_up_weight.shape[2]
    full_out = frozen_weight.shape[1]
    group_index = lax.axis_index("dp")
    tensor_index = lax.axis_index("tensor")
    capacity = CAP_OWN
    adapter_rows = adapter_store_row[sequence_adapter]
    owners = (adapter_rows // holder_count).reshape(group_total, slot_count)
    local_rows = (adapter_rows % holder_count).reshape(group_total, slot_count)
    slot_ids = jnp.arange(slot_count, dtype=jnp.int32)
    same_owner = owners[:, :, None] == owners[:, None, :]
    earlier_slot = slot_ids[None, :] < slot_ids[:, None]
    owner_rank = jnp.sum((same_owner & earlier_slot[None]).astype(jnp.int32), axis=2)
    cap_ids = jnp.arange(capacity, dtype=jnp.int32)
    owner_hits = (
        (owners == group_index)[:, :, None] & (owner_rank[:, :, None] == cap_ids[None, None, :])
    ).astype(jnp.float32)
    local_match = (
        local_rows[:, :, None] == jnp.arange(holder_count, dtype=jnp.int32)[None, None, :]
    ).astype(jnp.float32)
    selection = jnp.einsum("ejc,ejk->eck", owner_hits, local_match)
    mine_owner = lax.dynamic_index_in_dim(owners, group_index, 0, keepdims=False)
    mine_rank = lax.dynamic_index_in_dim(owner_rank, group_index, 0, keepdims=False)
    group_ids = jnp.arange(group_total, dtype=jnp.int32)
    pick_table = (
        (mine_owner[:, None] == group_ids[None, :])[:, :, None]
        & (mine_rank[:, None] == cap_ids[None, :])[:, None, :]
    ).astype(jnp.float32)
    live_sequence_mask = (slot_ids < group_live_counts[0]).astype(jnp.bfloat16)[:, None, None]
    rank = adapter_down_weight.shape[1]
    tensor_total = lax.axis_size("tensor")
    rows = slot_count * seq_length
    if (
        tensor_total > 1
        and output_portion % 128 == 0
        and dim_shard % output_portion == 0
        and rows % (16 * CHUNKS) == 0
        and full_out * dim_shard <= 1 << 22
    ):
        exchange = functools.partial(
            lax.all_to_all, axis_name="dp", split_axis=0, concat_axis=0, tiled=True
        )
        keep = selection.reshape(group_total * capacity, holder_count).astype(jnp.bfloat16)
        pick = pick_table.reshape(slot_count, group_total * capacity).astype(jnp.bfloat16)

        def bring(store):
            flat = store.reshape(holder_count, -1)
            chosen = jnp.dot(keep, flat, preferred_element_type=jnp.float32).astype(jnp.bfloat16)
            came = exchange(chosen.reshape(group_total, capacity, -1)).reshape(
                group_total * capacity, -1
            )
            mine = jnp.dot(pick, came, preferred_element_type=jnp.float32).astype(jnp.bfloat16)
            return mine.reshape(slot_count * rank, -1)

        def deliver(contribution):
            flat = contribution.reshape(slot_count, -1)
            sent = jnp.dot(pick.T, flat, preferred_element_type=jnp.float32).astype(jnp.bfloat16)
            came = exchange(sent.reshape(group_total, capacity, -1)).reshape(
                group_total * capacity, -1
            )
            stored = jnp.dot(keep.T, came, preferred_element_type=jnp.float32)
            return stored.reshape(holder_count, rank, -1)

        alive = (slot_ids < group_live_counts[0]).astype(jnp.float32)
        alive = jnp.broadcast_to(alive[:, None], (slot_count, seq_length)).reshape(rows, 1)
        key_value, grad_in, down_part, up_part = line_call(
            tensor_total,
            slot_count,
            activations.reshape(rows, dim_shard),
            frozen_weight,
            cotangent.reshape(rows, output_portion),
            alive,
            bring(adapter_down_weight),
            bring(adapter_up_weight),
        )
        return (
            key_value.reshape(slot_count, seq_length, output_portion),
            grad_in.reshape(slot_count, seq_length, dim_shard),
            deliver(down_part),
            deliver(up_part),
        )
    every_down, every_up = (
        lax.all_gather(adapter_down_weight, "dp", axis=0, tiled=True),
        lax.all_gather(adapter_up_weight, "dp", axis=0, tiled=True),
    )
    mine_rows = lax.dynamic_slice_in_dim(adapter_rows, group_index * slot_count, slot_count)
    one_hot = (
        mine_rows[:, None] == jnp.arange(group_total * holder_count, dtype=jnp.int32)[None, :]
    ).astype(jnp.bfloat16)
    down_weight_slice = jnp.einsum(
        "ja,ard->jrd", one_hot, every_down, preferred_element_type=jnp.float32
    ).astype(jnp.bfloat16)
    up_weight_slice = jnp.einsum(
        "ja,arw->jrw", one_hot, every_up, preferred_element_type=jnp.float32
    ).astype(jnp.bfloat16)
    low_sum = lax.psum(
        jnp.einsum(
            "cfy,cjy->cfj", activations, down_weight_slice, preferred_element_type=jnp.float32
        ).astype(jnp.bfloat16),
        "tensor",
    )
    partial_value = jnp.dot(
        activations.reshape(slot_count * seq_length, dim_shard),
        frozen_weight,
        preferred_element_type=jnp.float32,
    ).reshape(slot_count, seq_length, full_out)
    whole_sum = lax.psum(partial_value.astype(jnp.bfloat16), "tensor").astype(jnp.float32)
    frozen_output = lax.dynamic_slice_in_dim(
        whole_sum, tensor_index * output_portion, output_portion, 2
    )
    live_mask_float = live_sequence_mask.astype(jnp.float32)
    adapter_contribution = jnp.einsum(
        "slr,srw->slw", low_sum, up_weight_slice, preferred_element_type=jnp.float32
    )
    key_value_output = (
        (frozen_output + adapter_scale * adapter_contribution) * live_mask_float
    ).astype(jnp.bfloat16)
    masked = cotangent * live_sequence_mask
    masked_full = lax.all_gather(masked, "tensor", axis=2, tiled=True)
    back_sum = lax.psum(
        (
            adapter_scale
            * jnp.einsum(
                "bvg,bqg->bvq", masked, up_weight_slice, preferred_element_type=jnp.float32
            )
        ).astype(jnp.bfloat16),
        "tensor",
    )
    frozen_path = lax.dot_general(
        masked_full.reshape(slot_count * seq_length, full_out),
        frozen_weight,
        (((1,), (1,)), ((), ())),
        preferred_element_type=jnp.float32,
    )
    input_gradient = frozen_path.reshape(slot_count, seq_length, dim_shard) + jnp.einsum(
        "qip,qpb->qib", back_sum, down_weight_slice, preferred_element_type=jnp.float32
    )
    grad_input = (input_gradient * live_mask_float).astype(jnp.bfloat16)
    down_contributions = jnp.einsum(
        "ihn,ihx->inx", back_sum, activations, preferred_element_type=jnp.float32
    )
    up_contributions = adapter_scale * jnp.einsum(
        "tun,tuq->tnq", low_sum, masked, preferred_element_type=jnp.float32
    )
    send_grad_down = jnp.einsum(
        "joc,jrd->ocrd", pick_table, down_contributions, precision=lax.Precision.HIGHEST
    )
    send_grad_up = jnp.einsum(
        "joc,jrw->ocrw", pick_table, up_contributions, precision=lax.Precision.HIGHEST
    )
    back_down, back_up = (
        lax.all_to_all(
            send_grad_down.astype(jnp.bfloat16), "dp", split_axis=0, concat_axis=0, tiled=True
        ).astype(send_grad_down.dtype),
        lax.all_to_all(
            send_grad_up.astype(jnp.bfloat16), "dp", split_axis=0, concat_axis=0, tiled=True
        ).astype(send_grad_up.dtype),
    )
    grad_down = jnp.einsum("eck,ecrd->krd", selection, back_down, precision=lax.Precision.HIGHEST)
    grad_up = jnp.einsum("eck,ecrw->krw", selection, back_up, precision=lax.Precision.HIGHEST)
    return (key_value_output, grad_input, grad_down, grad_up)


def solution(mesh):
    in_specs = (
        P(("parts", "dp"), None, "tensor"),
        P("tensor", None),
        P(("parts", "dp"), None, "tensor"),
        P(("parts", "dp"), None, "tensor"),
        P(("parts", "dp"), None, "tensor"),
        P("parts"),
        P("parts"),
        P(("parts", "dp")),
    )
    out_specs = (
        P(("parts", "dp"), None, "tensor"),
        P(("parts", "dp"), None, "tensor"),
        P(("parts", "dp"), None, "tensor"),
        P(("parts", "dp"), None, "tensor"),
    )
    return jax.shard_map(shards, mesh=mesh, in_specs=in_specs, out_specs=out_specs, check_vma=False)
```

```python
import functools

import jax
import jax.numpy as jnp
from jax import lax
from jax.experimental import pallas as pl
from jax.experimental.pallas import tpu as pltpu
from jax.sharding import PartitionSpec as P

CAP_OWN = 2


adapter_scale = 2.0


CHUNKS = 4
MESH = pl.DeviceIdType.MESH
NT = (((1,), (1,)), ((), ()))
TN = (((0,), (0,)), ((), ()))


def line_kernel(
    n, groups, chunks, slots,
    x_hbm, w_hbm, cot_ref, alive_ref, store_down, store_up, keep_ref, pick_ref,
    kv_ref, gin_hbm, gdown_ref, gup_ref,
    panels, asked, came, given, landed, dp_send, dp_recv,
    x_ref, w_ref, full, part, from_left, from_right, acc, small, lowt, backt,
    load_sem, ag_recv, ag_right, ag_left, rs_recv_r, rs_recv_l, rs_send_r, rs_send_l,
    small_send, small_recv,
):
    me = lax.axis_index("tensor")
    rows, width = cot_ref.shape
    depth = x_ref.shape[1]
    rank = small.shape[1] // 2
    size = rows // chunks
    length = rows // slots
    last = n - 1
    mirror = last - me

    def chunk(c):
        return pl.ds(pl.multiple_of(c * size, size), size)

    def columns(d):
        return pl.ds(pl.multiple_of(d * width, width), width)

    def ag_copy(b, c, to_right):
        return pltpu.make_async_remote_copy(
            src_ref=full.at[b, chunk(c)],
            dst_ref=full.at[b, chunk(c)],
            send_sem=(ag_right if to_right else ag_left).at[b, c],
            recv_sem=ag_recv.at[b, c],
            device_id={"tensor": me + 1 if to_right else me - 1},
            device_id_type=MESH,
        )

    def rs_copy(d, c, to_right):
        return pltpu.make_async_remote_copy(
            src_ref=part.at[d, chunk(c)],
            dst_ref=(from_left if to_right else from_right).at[d, chunk(c)],
            send_sem=(rs_send_r if to_right else rs_send_l).at[d, c],
            recv_sem=(rs_recv_r if to_right else rs_recv_l).at[d, c],
            device_id={"tensor": me + 1 if to_right else me - 1},
            device_id_type=MESH,
        )

    def small_copy(peer, slot):
        return pltpu.make_async_remote_copy(
            src_ref=small.at[slot],
            dst_ref=small.at[slot],
            send_sem=small_send.at[peer],
            recv_sem=small_recv.at[slot],
            device_id={"tensor": peer},
            device_id_type=MESH,
        )

    group = lax.axis_index("dp")
    share = asked.shape[1]
    parts = depth // width
    down_ref = panels.at[:, pl.ds(0, depth)]
    up_ref = panels.at[:, pl.ds(depth, width)]

    def dp_copy(step, way, receiving):
        peer = lax.rem(group + step, groups)
        source, target = ((asked, came), (given, landed))[way]
        slot = peer if receiving else group
        return pltpu.make_async_remote_copy(
            src_ref=source.at[peer],
            dst_ref=target.at[slot],
            send_sem=dp_send.at[way, peer],
            recv_sem=dp_recv.at[way, slot],
            device_id={"dp": peer},
            device_id_type=MESH,
        )

    load_x = pltpu.make_async_copy(x_hbm, x_ref, load_sem.at[0])
    load_w = pltpu.make_async_copy(w_hbm, w_ref, load_sem.at[1])
    load_x.start()
    load_w.start()
    barrier = pltpu.get_barrier_semaphore()
    for step in range(1, n):
        pl.semaphore_signal(
            barrier, inc=1, device_id={"tensor": lax.rem(me + step, n)}, device_id_type=MESH
        )
    for step in range(1, groups):
        pl.semaphore_signal(
            barrier, inc=1, device_id={"dp": lax.rem(group + step, groups)}, device_id_type=MESH
        )
    full[me] = (cot_ref[...].astype(jnp.float32) * alive_ref[...]).astype(full.dtype)
    pl.semaphore_wait(barrier, n + groups - 2)

    @pl.loop(0, chunks)
    def _(c):
        @pl.when(me < last)
        def _():
            ag_copy(me, c, True).start()

        @pl.when(me > 0)
        def _():
            ag_copy(me, c, False).start()

    for j in range(parts + 1):
        if j < parts:
            store = store_down[:, j * width : (j + 1) * width]
        else:
            store = store_up[...]
        chosen = jnp.dot(
            keep_ref[...], store, preferred_element_type=jnp.float32
        ).astype(asked.dtype)
        for e in range(groups):
            asked[e, :, j * width : (j + 1) * width] = chosen[e * share : (e + 1) * share]
    for step in range(1, groups):
        dp_copy(step, 0, False).start()
    came[group] = asked[group]

    shape = (slots * rank, rows)
    slot_of_row = lax.broadcasted_iota(jnp.int32, shape, 0) // rank
    slot_of_column = lax.broadcasted_iota(jnp.int32, shape, 1) // length
    diagonal = slot_of_row == slot_of_column

    def compact(wide):
        wide = jnp.where(diagonal, wide, 0.0)
        total = wide[0:rank]
        for s in range(1, slots):
            total = total + wide[s * rank : (s + 1) * rank]
        return total

    load_x.wait()
    load_w.wait()

    @pl.loop(0, n)
    def _(k):
        d = jnp.where(me == 0, last - k, k)

        @pl.loop(0, chunks)
        def _(c):
            part[d, chunk(c), :] = jnp.dot(
                x_ref[chunk(c), :], w_ref[:, columns(d)], preferred_element_type=jnp.float32
            ).astype(part.dtype)

            @pl.when((me == 0) & (d > 0))
            def _():
                rs_copy(d, c, True).start()

            @pl.when((me == last) & (d < last))
            def _():
                rs_copy(d, c, False).start()

    for step in range(1, groups):
        dp_copy(step, 0, True).wait_recv()
    for j in range(parts + 1):
        block = came[:, :, j * width : (j + 1) * width].reshape(groups * share, width)
        panels[:, j * width : (j + 1) * width] = jnp.dot(
            pick_ref[...], block, preferred_element_type=jnp.float32
        ).astype(panels.dtype)
    back_part = compact(
        lax.dot_general(up_ref[...], full[me], NT, preferred_element_type=jnp.float32)
    )
    small[me, rank:, :] = (adapter_scale * back_part).astype(small.dtype)
    low_part = compact(
        lax.dot_general(down_ref[...], x_ref[...], NT, preferred_element_type=jnp.float32)
    )
    small[me, :rank, :] = low_part.astype(small.dtype)
    for step in range(1, n):
        small_copy(lax.rem(me + step, n), me).start()

    def frozen(b, first):
        @pl.loop(0, chunks)
        def _(c):
            @pl.loop(0, depth // width)
            def _(j):
                piece = lax.dot_general(
                    full[b, chunk(c), :],
                    w_ref[columns(j), columns(b)],
                    NT,
                    preferred_element_type=jnp.float32,
                )
                if first:
                    acc[chunk(c), columns(j)] = piece
                else:
                    acc[chunk(c), columns(j)] += piece

    frozen(me, True)

    def receive(q, c):
        @pl.when(q < me)
        def _():
            b = me - 1 - q
            ag_copy(b, c, True).wait_recv()

            @pl.when(me < last)
            def _():
                ag_copy(b, c, True).start()

        @pl.when((q >= me) & (me > 0))
        def _():
            d = last - (q - me)
            rs_copy(d, c, True).wait_recv()
            part[d, chunk(c), :] = (
                part[d, chunk(c), :].astype(jnp.float32)
                + from_left[d, chunk(c), :].astype(jnp.float32)
            ).astype(part.dtype)
            rs_copy(d, c, True).start()

        @pl.when(q < mirror)
        def _():
            b = me + 1 + q
            ag_copy(b, c, False).wait_recv()

            @pl.when(me > 0)
            def _():
                ag_copy(b, c, False).start()

        @pl.when((q >= mirror) & (me < last))
        def _():
            d = q - mirror
            rs_copy(d, c, False).wait_recv()
            part[d, chunk(c), :] = (
                part[d, chunk(c), :].astype(jnp.float32)
                + from_right[d, chunk(c), :].astype(jnp.float32)
            ).astype(part.dtype)
            rs_copy(d, c, False).start()

    def round_of(q):
        @pl.loop(0, chunks)
        def _(c):
            receive(q, c)

        @pl.when(q < me)
        def _():
            frozen(me - 1 - q, False)

        @pl.when(q < mirror)
        def _():
            frozen(me + 1 + q, False)

    @pl.loop(0, last - 1)
    def _(q):
        round_of(q)

    for step in range(1, n):
        source = lax.rem(me + step, n)
        small_copy(source, source).wait_recv()
    total = small[0].astype(jnp.float32)
    for b in range(1, n):
        total = total + small[b].astype(jnp.float32)
    low = jnp.where(diagonal, jnp.concatenate([total[:rank]] * slots, axis=0), 0.0)
    back = jnp.where(diagonal, jnp.concatenate([total[rank:]] * slots, axis=0), 0.0)
    lowt[...] = low.astype(lowt.dtype)
    backt[...] = back.astype(backt.dtype)
    for j in range(parts + 1):
        if j < parts:
            block = jnp.dot(
                backt[...],
                x_ref[:, j * width : (j + 1) * width],
                preferred_element_type=jnp.float32,
            )
        else:
            block = adapter_scale * jnp.dot(
                lowt[...], full[me], preferred_element_type=jnp.float32
            )
        block = lax.dot_general(
            pick_ref[...], block.astype(given.dtype), TN, preferred_element_type=jnp.float32
        ).astype(given.dtype)
        for e in range(groups):
            given[e, :, j * width : (j + 1) * width] = block[e * share : (e + 1) * share]
    for step in range(1, groups):
        dp_copy(step, 1, False).start()
    landed[group] = given[group]

    round_of(last - 1)

    @pl.loop(0, parts)
    def _(j):
        x_ref[:, columns(j)] = (
            alive_ref[...]
            * (
                acc[:, columns(j)]
                + lax.dot_general(
                    backt[...], panels[:, columns(j)], TN, preferred_element_type=jnp.float32
                )
            )
        ).astype(x_ref.dtype)

    store_x = pltpu.make_async_copy(x_ref, gin_hbm, load_sem.at[2])
    store_x.start()
    for step in range(1, groups):
        dp_copy(step, 1, True).wait_recv()
    for j in range(parts + 1):
        block = landed[:, :, j * width : (j + 1) * width].reshape(groups * share, width)
        block = lax.dot_general(
            keep_ref[...], block, TN, preferred_element_type=jnp.float32
        )
        if j < parts:
            gdown_ref[:, j * width : (j + 1) * width] = block
        else:
            gup_ref[...] = block

    acc[:, :width] = adapter_scale * lax.dot_general(
        lowt[...], up_ref[...], TN, preferred_element_type=jnp.float32
    )

    def rs_finish(c, to_right):
        rs_copy(me, c, to_right).wait_recv()
        arrived = from_left if to_right else from_right
        acc[chunk(c), :width] += arrived[me, chunk(c), :].astype(jnp.float32)

    @pl.loop(0, chunks)
    def _(c):
        acc[chunk(c), :width] += part[me, chunk(c), :].astype(jnp.float32)

        @pl.when(me > 0)
        def _():
            rs_finish(c, True)

        @pl.when(me < last)
        def _():
            rs_finish(c, False)

        kv_ref[chunk(c), :] = (alive_ref[chunk(c), :] * acc[chunk(c), :width]).astype(kv_ref.dtype)

    def drain(b, c):
        @pl.when((b <= me) & (me < last))
        def _():
            ag_copy(b, c, True).wait_send()

        @pl.when((b >= me) & (me > 0))
        def _():
            ag_copy(b, c, False).wait_send()

        @pl.when(b > me)
        def _():
            rs_copy(b, c, True).wait_send()

        @pl.when(b < me)
        def _():
            rs_copy(b, c, False).wait_send()

    for step in range(1, n):
        small_copy(lax.rem(me + step, n), me).wait_send()
    for step in range(1, groups):
        dp_copy(step, 0, False).wait_send()
        dp_copy(step, 1, False).wait_send()
    store_x.wait()

    @pl.loop(0, n)
    def _(b):
        @pl.loop(0, chunks)
        def _(c):
            drain(b, c)


def line_call(n, groups, slots, x, w, cot, alive, down, up, keep, pick):
    rows, depth = x.shape
    width = cot.shape[1]
    held = down.shape[0]
    panel = pick.shape[0]
    rank = panel // slots
    share = keep.shape[0] // groups
    bf16 = jnp.bfloat16
    vmem = pl.BlockSpec(memory_space=pltpu.VMEM)
    hbm = pl.BlockSpec(memory_space=pl.ANY)
    dma = pltpu.SemaphoreType.DMA((n, CHUNKS))
    return pl.pallas_call(
        functools.partial(line_kernel, n, groups, CHUNKS, slots),
        out_shape=(
            jax.ShapeDtypeStruct((rows, width), bf16),
            jax.ShapeDtypeStruct((rows, depth), bf16),
            jax.ShapeDtypeStruct((held, depth), jnp.float32),
            jax.ShapeDtypeStruct((held, width), jnp.float32),
        ),
        in_specs=[hbm, hbm, vmem, vmem, vmem, vmem, vmem, vmem],
        out_specs=(vmem, hbm, vmem, vmem),
        scratch_shapes=[
            pltpu.VMEM((panel, depth + width), bf16),
            pltpu.VMEM((groups, share, depth + width), bf16),
            pltpu.VMEM((groups, share, depth + width), bf16),
            pltpu.VMEM((groups, share, depth + width), bf16),
            pltpu.VMEM((groups, share, depth + width), bf16),
            pltpu.SemaphoreType.DMA((2, groups)),
            pltpu.SemaphoreType.DMA((2, groups)),
            pltpu.VMEM((rows, depth), bf16),
            pltpu.VMEM(w.shape, bf16),
            pltpu.VMEM((n, rows, width), bf16),
            pltpu.VMEM((n, rows, width), bf16),
            pltpu.VMEM((n, rows, width), bf16),
            pltpu.VMEM((n, rows, width), bf16),
            pltpu.VMEM((rows, depth), jnp.float32),
            pltpu.VMEM((n, 2 * rank, rows), bf16),
            pltpu.VMEM((panel, rows), bf16),
            pltpu.VMEM((panel, rows), bf16),
            pltpu.SemaphoreType.DMA((3,)),
            dma, dma, dma, dma, dma, dma, dma,
            pltpu.SemaphoreType.DMA((n,)),
            pltpu.SemaphoreType.DMA((n,)),
        ],
        compiler_params=pltpu.CompilerParams(
            collective_id=0, has_side_effects=True, vmem_limit_bytes=60 << 20
        ),
        cost_estimate=pl.CostEstimate(
            flops=4 * rows * depth * n * width, bytes_accessed=30_000_000, transcendentals=0
        ),
    )(x, w, cot, alive, down, up, keep, pick)


def shards(
    activations,
    frozen_weight,
    cotangent,
    adapter_down_weight,
    adapter_up_weight,
    sequence_adapter,
    adapter_store_row,
    group_live_counts,
):
    group_total = lax.axis_size("dp")
    slot_count, seq_length, dim_shard = activations.shape
    holder_count = adapter_down_weight.shape[0]
    output_portion = adapter_up_weight.shape[2]
    full_out = frozen_weight.shape[1]
    group_index = lax.axis_index("dp")
    tensor_index = lax.axis_index("tensor")
    capacity = CAP_OWN
    adapter_rows = adapter_store_row[sequence_adapter]
    owners = (adapter_rows // holder_count).reshape(group_total, slot_count)
    local_rows = (adapter_rows % holder_count).reshape(group_total, slot_count)
    slot_ids = jnp.arange(slot_count, dtype=jnp.int32)
    same_owner = owners[:, :, None] == owners[:, None, :]
    earlier_slot = slot_ids[None, :] < slot_ids[:, None]
    owner_rank = jnp.sum((same_owner & earlier_slot[None]).astype(jnp.int32), axis=2)
    cap_ids = jnp.arange(capacity, dtype=jnp.int32)
    owner_hits = (
        (owners == group_index)[:, :, None] & (owner_rank[:, :, None] == cap_ids[None, None, :])
    ).astype(jnp.float32)
    local_match = (
        local_rows[:, :, None] == jnp.arange(holder_count, dtype=jnp.int32)[None, None, :]
    ).astype(jnp.float32)
    selection = jnp.einsum("ejc,ejk->eck", owner_hits, local_match)
    mine_owner = lax.dynamic_index_in_dim(owners, group_index, 0, keepdims=False)
    mine_rank = lax.dynamic_index_in_dim(owner_rank, group_index, 0, keepdims=False)
    group_ids = jnp.arange(group_total, dtype=jnp.int32)
    pick_table = (
        (mine_owner[:, None] == group_ids[None, :])[:, :, None]
        & (mine_rank[:, None] == cap_ids[None, :])[:, None, :]
    ).astype(jnp.float32)
    live_sequence_mask = (slot_ids < group_live_counts[0]).astype(jnp.bfloat16)[:, None, None]
    rank = adapter_down_weight.shape[1]
    tensor_total = lax.axis_size("tensor")
    rows = slot_count * seq_length
    if (
        tensor_total > 1
        and output_portion % 128 == 0
        and dim_shard % output_portion == 0
        and rows % (16 * CHUNKS) == 0
        and rank % 16 == 0
        and group_total > 1
        and full_out * dim_shard <= 1 << 22
    ):
        keep = selection.reshape(group_total * capacity, holder_count).astype(jnp.bfloat16)
        pick = pick_table.reshape(slot_count, group_total * capacity).astype(jnp.bfloat16)

        def widen(table):
            down, across = table.shape
            unit = jnp.eye(rank, dtype=table.dtype)
            wide = table[:, None, :, None] * unit[None, :, None, :]
            return wide.reshape(down * rank, across * rank)

        alive = (slot_ids < group_live_counts[0]).astype(jnp.float32)
        alive = jnp.broadcast_to(alive[:, None], (slot_count, seq_length)).reshape(rows, 1)
        key_value, grad_in, down_part, up_part = line_call(
            tensor_total,
            group_total,
            slot_count,
            activations.reshape(rows, dim_shard),
            frozen_weight,
            cotangent.reshape(rows, output_portion),
            alive,
            adapter_down_weight.reshape(holder_count * rank, dim_shard),
            adapter_up_weight.reshape(holder_count * rank, output_portion),
            widen(keep),
            widen(pick),
        )
        return (
            key_value.reshape(slot_count, seq_length, output_portion),
            grad_in.reshape(slot_count, seq_length, dim_shard),
            down_part.reshape(holder_count, rank, dim_shard),
            up_part.reshape(holder_count, rank, output_portion),
        )
    every_down, every_up = (
        lax.all_gather(adapter_down_weight, "dp", axis=0, tiled=True),
        lax.all_gather(adapter_up_weight, "dp", axis=0, tiled=True),
    )
    mine_rows = lax.dynamic_slice_in_dim(adapter_rows, group_index * slot_count, slot_count)
    one_hot = (
        mine_rows[:, None] == jnp.arange(group_total * holder_count, dtype=jnp.int32)[None, :]
    ).astype(jnp.bfloat16)
    down_weight_slice = jnp.einsum(
        "ja,ard->jrd", one_hot, every_down, preferred_element_type=jnp.float32
    ).astype(jnp.bfloat16)
    up_weight_slice = jnp.einsum(
        "ja,arw->jrw", one_hot, every_up, preferred_element_type=jnp.float32
    ).astype(jnp.bfloat16)
    low_sum = lax.psum(
        jnp.einsum(
            "cfy,cjy->cfj", activations, down_weight_slice, preferred_element_type=jnp.float32
        ).astype(jnp.bfloat16),
        "tensor",
    )
    partial_value = jnp.dot(
        activations.reshape(slot_count * seq_length, dim_shard),
        frozen_weight,
        preferred_element_type=jnp.float32,
    ).reshape(slot_count, seq_length, full_out)
    whole_sum = lax.psum(partial_value.astype(jnp.bfloat16), "tensor").astype(jnp.float32)
    frozen_output = lax.dynamic_slice_in_dim(
        whole_sum, tensor_index * output_portion, output_portion, 2
    )
    live_mask_float = live_sequence_mask.astype(jnp.float32)
    adapter_contribution = jnp.einsum(
        "slr,srw->slw", low_sum, up_weight_slice, preferred_element_type=jnp.float32
    )
    key_value_output = (
        (frozen_output + adapter_scale * adapter_contribution) * live_mask_float
    ).astype(jnp.bfloat16)
    masked = cotangent * live_sequence_mask
    masked_full = lax.all_gather(masked, "tensor", axis=2, tiled=True)
    back_sum = lax.psum(
        (
            adapter_scale
            * jnp.einsum(
                "bvg,bqg->bvq", masked, up_weight_slice, preferred_element_type=jnp.float32
            )
        ).astype(jnp.bfloat16),
        "tensor",
    )
    frozen_path = lax.dot_general(
        masked_full.reshape(slot_count * seq_length, full_out),
        frozen_weight,
        (((1,), (1,)), ((), ())),
        preferred_element_type=jnp.float32,
    )
    input_gradient = frozen_path.reshape(slot_count, seq_length, dim_shard) + jnp.einsum(
        "qip,qpb->qib", back_sum, down_weight_slice, preferred_element_type=jnp.float32
    )
    grad_input = (input_gradient * live_mask_float).astype(jnp.bfloat16)
    down_contributions = jnp.einsum(
        "ihn,ihx->inx", back_sum, activations, preferred_element_type=jnp.float32
    )
    up_contributions = adapter_scale * jnp.einsum(
        "tun,tuq->tnq", low_sum, masked, preferred_element_type=jnp.float32
    )
    send_grad_down = jnp.einsum(
        "joc,jrd->ocrd", pick_table, down_contributions, precision=lax.Precision.HIGHEST
    )
    send_grad_up = jnp.einsum(
        "joc,jrw->ocrw", pick_table, up_contributions, precision=lax.Precision.HIGHEST
    )
    back_down, back_up = (
        lax.all_to_all(
            send_grad_down.astype(jnp.bfloat16), "dp", split_axis=0, concat_axis=0, tiled=True
        ).astype(send_grad_down.dtype),
        lax.all_to_all(
            send_grad_up.astype(jnp.bfloat16), "dp", split_axis=0, concat_axis=0, tiled=True
        ).astype(send_grad_up.dtype),
    )
    grad_down = jnp.einsum("eck,ecrd->krd", selection, back_down, precision=lax.Precision.HIGHEST)
    grad_up = jnp.einsum("eck,ecrw->krw", selection, back_up, precision=lax.Precision.HIGHEST)
    return (key_value_output, grad_input, grad_down, grad_up)


def solution(mesh):
    in_specs = (
        P(("parts", "dp"), None, "tensor"),
        P("tensor", None),
        P(("parts", "dp"), None, "tensor"),
        P(("parts", "dp"), None, "tensor"),
        P(("parts", "dp"), None, "tensor"),
        P("parts"),
        P("parts"),
        P(("parts", "dp")),
    )
    out_specs = (
        P(("parts", "dp"), None, "tensor"),
        P(("parts", "dp"), None, "tensor"),
        P(("parts", "dp"), None, "tensor"),
        P(("parts", "dp"), None, "tensor"),
    )
    return jax.shard_map(shards, mesh=mesh, in_specs=in_specs, out_specs=out_specs, check_vma=False)
```

```python
import functools

import jax
import jax.numpy as jnp
from jax import lax
from jax.experimental import pallas as pl
from jax.experimental.pallas import tpu as pltpu
from jax.sharding import PartitionSpec as P

CAP_OWN = 2


adapter_scale = 2.0


CHUNKS = 4
MESH = pl.DeviceIdType.MESH
NT = (((1,), (1,)), ((), ()))
TN = (((0,), (0,)), ((), ()))


def line_kernel(
    n, groups, chunks, slots,
    x_hbm, w_hbm, cot_ref, live_ref, store_down, store_up, keep_ref, pick_ref,
    kv_ref, gin_hbm, back_ref, up_back_ref,
    alive_ref, panels, asked, came, given, landed, dp_send, dp_recv,
    x_ref, w_ref, full, part, from_left, from_right, acc, small, lowt, backt,
    load_sem, ag_recv, ag_right, ag_left, rs_recv_r, rs_recv_l, rs_send_r, rs_send_l,
    small_send, small_recv,
):
    me = lax.axis_index("tensor")
    rows, width = cot_ref.shape
    depth = x_ref.shape[1]
    rank = small.shape[1] // 2
    size = rows // chunks
    length = rows // slots
    last = n - 1
    mirror = last - me

    def chunk(c):
        return pl.ds(pl.multiple_of(c * size, size), size)

    def columns(d):
        return pl.ds(pl.multiple_of(d * width, width), width)

    def ag_copy(b, c, to_right):
        return pltpu.make_async_remote_copy(
            src_ref=full.at[b, chunk(c)],
            dst_ref=full.at[b, chunk(c)],
            send_sem=(ag_right if to_right else ag_left).at[b, c],
            recv_sem=ag_recv.at[b, c],
            device_id={"tensor": me + 1 if to_right else me - 1},
            device_id_type=MESH,
        )

    def rs_copy(d, c, to_right):
        return pltpu.make_async_remote_copy(
            src_ref=part.at[d, chunk(c)],
            dst_ref=(from_left if to_right else from_right).at[d, chunk(c)],
            send_sem=(rs_send_r if to_right else rs_send_l).at[d, c],
            recv_sem=(rs_recv_r if to_right else rs_recv_l).at[d, c],
            device_id={"tensor": me + 1 if to_right else me - 1},
            device_id_type=MESH,
        )

    def small_copy(peer, slot):
        return pltpu.make_async_remote_copy(
            src_ref=small.at[slot],
            dst_ref=small.at[slot],
            send_sem=small_send.at[peer],
            recv_sem=small_recv.at[slot],
            device_id={"tensor": peer},
            device_id_type=MESH,
        )

    group = lax.axis_index("dp")
    share = asked.shape[1]
    parts = depth // width
    down_ref = panels.at[:, pl.ds(0, depth)]
    up_ref = panels.at[:, pl.ds(depth, width)]

    def dp_copy(step, way, receiving):
        peer = lax.rem(group + step, groups)
        source, target = ((asked, came), (given, landed))[way]
        slot = peer if receiving else group
        return pltpu.make_async_remote_copy(
            src_ref=source.at[peer],
            dst_ref=target.at[slot],
            send_sem=dp_send.at[way, peer],
            recv_sem=dp_recv.at[way, slot],
            device_id={"dp": peer},
            device_id_type=MESH,
        )

    load_x = pltpu.make_async_copy(x_hbm, x_ref, load_sem.at[0])
    load_w = pltpu.make_async_copy(w_hbm, w_ref, load_sem.at[1])
    load_x.start()
    load_w.start()
    barrier = pltpu.get_barrier_semaphore()
    for step in range(1, n):
        pl.semaphore_signal(
            barrier, inc=1, device_id={"tensor": lax.rem(me + step, n)}, device_id_type=MESH
        )
    for step in range(1, groups):
        pl.semaphore_signal(
            barrier, inc=1, device_id={"dp": lax.rem(group + step, groups)}, device_id_type=MESH
        )
    alive_ref[...] = jnp.concatenate(
        [jnp.broadcast_to(live_ref[s : s + 1, :1], (length, 1)) for s in range(slots)], axis=0
    )
    full[me] = (cot_ref[...].astype(jnp.float32) * alive_ref[...]).astype(full.dtype)
    for j in range(parts + 1):
        if j < parts:
            store = store_down[:, j * width : (j + 1) * width]
        else:
            store = store_up[...]
        chosen = jnp.dot(
            keep_ref[...], store, preferred_element_type=jnp.float32
        ).astype(asked.dtype)
        for e in range(groups):
            asked[e, :, j * width : (j + 1) * width] = chosen[e * share : (e + 1) * share]
    pl.semaphore_wait(barrier, n + groups - 2)
    for step in range(1, groups):
        dp_copy(step, 0, False).start()
    came[group] = asked[group]


    @pl.loop(0, chunks)
    def _(c):
        @pl.when(me < last)
        def _():
            ag_copy(me, c, True).start()

        @pl.when(me > 0)
        def _():
            ag_copy(me, c, False).start()

    shape = (slots * rank, rows)
    slot_of_row = lax.broadcasted_iota(jnp.int32, shape, 0) // rank
    slot_of_column = lax.broadcasted_iota(jnp.int32, shape, 1) // length
    diagonal = slot_of_row == slot_of_column

    def compact(wide):
        wide = jnp.where(diagonal, wide, 0.0)
        total = wide[0:rank]
        for s in range(1, slots):
            total = total + wide[s * rank : (s + 1) * rank]
        return total

    load_x.wait()
    load_w.wait()

    @pl.loop(0, n)
    def _(k):
        d = jnp.where(me == 0, last - k, k)

        @pl.loop(0, chunks)
        def _(c):
            part[d, chunk(c), :] = jnp.dot(
                x_ref[chunk(c), :], w_ref[:, columns(d)], preferred_element_type=jnp.float32
            ).astype(part.dtype)

            @pl.when((me == 0) & (d > 0))
            def _():
                rs_copy(d, c, True).start()

            @pl.when((me == last) & (d < last))
            def _():
                rs_copy(d, c, False).start()

    for step in range(1, groups):
        dp_copy(step, 0, True).wait_recv()
    for j in range(parts + 1):
        block = came[:, :, j * width : (j + 1) * width].reshape(groups * share, width)
        panels[:, j * width : (j + 1) * width] = jnp.dot(
            pick_ref[...], block, preferred_element_type=jnp.float32
        ).astype(panels.dtype)
    back_part = compact(
        lax.dot_general(up_ref[...], full[me], NT, preferred_element_type=jnp.float32)
    )
    small[me, rank:, :] = (adapter_scale * back_part).astype(small.dtype)
    low_part = compact(
        lax.dot_general(down_ref[...], x_ref[...], NT, preferred_element_type=jnp.float32)
    )
    small[me, :rank, :] = low_part.astype(small.dtype)
    for step in range(1, n):
        small_copy(lax.rem(me + step, n), me).start()

    def frozen(b, first):
        @pl.loop(0, chunks)
        def _(c):
            @pl.loop(0, depth // width)
            def _(j):
                piece = lax.dot_general(
                    full[b, chunk(c), :],
                    w_ref[columns(j), columns(b)],
                    NT,
                    preferred_element_type=jnp.float32,
                )
                if first:
                    acc[chunk(c), columns(j)] = piece
                else:
                    acc[chunk(c), columns(j)] += piece

    def receive(q, c):
        @pl.when(q < me)
        def _():
            b = me - 1 - q
            ag_copy(b, c, True).wait_recv()

            @pl.when(me < last)
            def _():
                ag_copy(b, c, True).start()

        @pl.when((q >= me) & (me > 0))
        def _():
            d = last - (q - me)
            rs_copy(d, c, True).wait_recv()
            part[d, chunk(c), :] = (
                part[d, chunk(c), :].astype(jnp.float32)
                + from_left[d, chunk(c), :].astype(jnp.float32)
            ).astype(part.dtype)
            rs_copy(d, c, True).start()

        @pl.when(q < mirror)
        def _():
            b = me + 1 + q
            ag_copy(b, c, False).wait_recv()

            @pl.when(me > 0)
            def _():
                ag_copy(b, c, False).start()

        @pl.when((q >= mirror) & (me < last))
        def _():
            d = q - mirror
            rs_copy(d, c, False).wait_recv()
            part[d, chunk(c), :] = (
                part[d, chunk(c), :].astype(jnp.float32)
                + from_right[d, chunk(c), :].astype(jnp.float32)
            ).astype(part.dtype)
            rs_copy(d, c, False).start()

    def arrivals(q):
        @pl.loop(0, chunks)
        def _(c):
            receive(q, c)

    def products(q):
        @pl.when(q < me)
        def _():
            frozen(me - 1 - q, False)

        @pl.when(q < mirror)
        def _():
            frozen(me + 1 + q, False)

    arrivals(0)
    frozen(me, True)
    products(0)

    for step in range(1, n):
        source = lax.rem(me + step, n)
        small_copy(source, source).wait_recv()
    total = small[0].astype(jnp.float32)
    for b in range(1, n):
        total = total + small[b].astype(jnp.float32)
    low = jnp.where(diagonal, jnp.concatenate([total[:rank]] * slots, axis=0), 0.0)
    back = jnp.where(diagonal, jnp.concatenate([total[rank:]] * slots, axis=0), 0.0)
    lowt[...] = low.astype(lowt.dtype)
    backt[...] = back.astype(backt.dtype)
    for j in range(parts + 1):
        if j < parts:
            block = jnp.dot(
                backt[...],
                x_ref[:, j * width : (j + 1) * width],
                preferred_element_type=jnp.float32,
            )
        else:
            block = adapter_scale * jnp.dot(
                lowt[...], full[me], preferred_element_type=jnp.float32
            )
        block = lax.dot_general(
            pick_ref[...], block.astype(given.dtype), TN, preferred_element_type=jnp.float32
        ).astype(given.dtype)
        for e in range(groups):
            given[e, :, j * width : (j + 1) * width] = block[e * share : (e + 1) * share]
    for step in range(1, groups):
        dp_copy(step, 1, False).start()
    landed[group] = given[group]

    @pl.loop(1, last)
    def _(q):
        arrivals(q)
        products(q)

    @pl.loop(0, parts)
    def _(j):
        x_ref[:, columns(j)] = (
            alive_ref[...]
            * (
                acc[:, columns(j)]
                + lax.dot_general(
                    backt[...], panels[:, columns(j)], TN, preferred_element_type=jnp.float32
                )
            )
        ).astype(x_ref.dtype)

    store_x = pltpu.make_async_copy(x_ref, gin_hbm, load_sem.at[2])
    store_x.start()
    for step in range(1, groups):
        dp_copy(step, 1, True).wait_recv()
    back_ref[...] = landed[:, :, :depth].reshape(back_ref.shape)
    up_back_ref[...] = landed[:, :, depth:].reshape(up_back_ref.shape)

    acc[:, :width] = adapter_scale * lax.dot_general(
        lowt[...], up_ref[...], TN, preferred_element_type=jnp.float32
    )

    def rs_finish(c, to_right):
        rs_copy(me, c, to_right).wait_recv()
        arrived = from_left if to_right else from_right
        acc[chunk(c), :width] += arrived[me, chunk(c), :].astype(jnp.float32)

    @pl.loop(0, chunks)
    def _(c):
        acc[chunk(c), :width] += part[me, chunk(c), :].astype(jnp.float32)

        @pl.when(me > 0)
        def _():
            rs_finish(c, True)

        @pl.when(me < last)
        def _():
            rs_finish(c, False)

        kv_ref[chunk(c), :] = (alive_ref[chunk(c), :] * acc[chunk(c), :width]).astype(kv_ref.dtype)

    def drain(b, c):
        @pl.when((b <= me) & (me < last))
        def _():
            ag_copy(b, c, True).wait_send()

        @pl.when((b >= me) & (me > 0))
        def _():
            ag_copy(b, c, False).wait_send()

        @pl.when(b > me)
        def _():
            rs_copy(b, c, True).wait_send()

        @pl.when(b < me)
        def _():
            rs_copy(b, c, False).wait_send()

    for step in range(1, n):
        small_copy(lax.rem(me + step, n), me).wait_send()
    for step in range(1, groups):
        dp_copy(step, 0, False).wait_send()
        dp_copy(step, 1, False).wait_send()
    store_x.wait()

    @pl.loop(0, n)
    def _(b):
        @pl.loop(0, chunks)
        def _(c):
            drain(b, c)


def line_call(n, groups, slots, x, w, cot, alive, down, up, keep, pick):
    rows, depth = x.shape
    width = cot.shape[1]
    panel = pick.shape[0]
    rank = panel // slots
    share = keep.shape[0] // groups
    bf16 = jnp.bfloat16
    vmem = pl.BlockSpec(memory_space=pltpu.VMEM)
    hbm = pl.BlockSpec(memory_space=pl.ANY)
    dma = pltpu.SemaphoreType.DMA((n, CHUNKS))
    return pl.pallas_call(
        functools.partial(line_kernel, n, groups, CHUNKS, slots),
        out_shape=(
            jax.ShapeDtypeStruct((rows, width), bf16),
            jax.ShapeDtypeStruct((rows, depth), bf16),
            jax.ShapeDtypeStruct((keep.shape[0], depth), bf16),
            jax.ShapeDtypeStruct((keep.shape[0], width), bf16),
        ),
        in_specs=[hbm, hbm, vmem, vmem, vmem, vmem, vmem, vmem],
        out_specs=(vmem, hbm, vmem, vmem),
        scratch_shapes=[
            pltpu.VMEM((rows, 1), jnp.float32),
            pltpu.VMEM((panel, depth + width), bf16),
            pltpu.VMEM((groups, share, depth + width), bf16),
            pltpu.VMEM((groups, share, depth + width), bf16),
            pltpu.VMEM((groups, share, depth + width), bf16),
            pltpu.VMEM((groups, share, depth + width), bf16),
            pltpu.SemaphoreType.DMA((2, groups)),
            pltpu.SemaphoreType.DMA((2, groups)),
            pltpu.VMEM((rows, depth), bf16),
            pltpu.VMEM(w.shape, bf16),
            pltpu.VMEM((n, rows, width), bf16),
            pltpu.VMEM((n, rows, width), bf16),
            pltpu.VMEM((n, rows, width), bf16),
            pltpu.VMEM((n, rows, width), bf16),
            pltpu.VMEM((rows, depth), jnp.float32),
            pltpu.VMEM((n, 2 * rank, rows), bf16),
            pltpu.VMEM((panel, rows), bf16),
            pltpu.VMEM((panel, rows), bf16),
            pltpu.SemaphoreType.DMA((3,)),
            dma, dma, dma, dma, dma, dma, dma,
            pltpu.SemaphoreType.DMA((n,)),
            pltpu.SemaphoreType.DMA((n,)),
        ],
        compiler_params=pltpu.CompilerParams(
            collective_id=0, has_side_effects=True, vmem_limit_bytes=60 << 20
        ),
        cost_estimate=pl.CostEstimate(
            flops=4 * rows * depth * n * width, bytes_accessed=30_000_000, transcendentals=0
        ),
    )(x, w, cot, alive, down, up, keep, pick)


def shards(
    activations,
    frozen_weight,
    cotangent,
    adapter_down_weight,
    adapter_up_weight,
    sequence_adapter,
    adapter_store_row,
    group_live_counts,
):
    group_total = lax.axis_size("dp")
    slot_count, seq_length, dim_shard = activations.shape
    holder_count = adapter_down_weight.shape[0]
    output_portion = adapter_up_weight.shape[2]
    full_out = frozen_weight.shape[1]
    group_index = lax.axis_index("dp")
    tensor_index = lax.axis_index("tensor")
    capacity = CAP_OWN
    adapter_rows = adapter_store_row[sequence_adapter]
    owners = (adapter_rows // holder_count).reshape(group_total, slot_count)
    local_rows = (adapter_rows % holder_count).reshape(group_total, slot_count)
    slot_ids = jnp.arange(slot_count, dtype=jnp.int32)
    same_owner = owners[:, :, None] == owners[:, None, :]
    earlier_slot = slot_ids[None, :] < slot_ids[:, None]
    owner_rank = jnp.sum((same_owner & earlier_slot[None]).astype(jnp.int32), axis=2)
    cap_ids = jnp.arange(capacity, dtype=jnp.int32)
    owner_hits = (
        (owners == group_index)[:, :, None] & (owner_rank[:, :, None] == cap_ids[None, None, :])
    ).astype(jnp.float32)
    local_match = (
        local_rows[:, :, None] == jnp.arange(holder_count, dtype=jnp.int32)[None, None, :]
    ).astype(jnp.float32)
    selection = jnp.einsum("ejc,ejk->eck", owner_hits, local_match)
    mine_owner = lax.dynamic_index_in_dim(owners, group_index, 0, keepdims=False)
    mine_rank = lax.dynamic_index_in_dim(owner_rank, group_index, 0, keepdims=False)
    group_ids = jnp.arange(group_total, dtype=jnp.int32)
    pick_table = (
        (mine_owner[:, None] == group_ids[None, :])[:, :, None]
        & (mine_rank[:, None] == cap_ids[None, :])[:, None, :]
    ).astype(jnp.float32)
    live_sequence_mask = (slot_ids < group_live_counts[0]).astype(jnp.bfloat16)[:, None, None]
    rank = adapter_down_weight.shape[1]
    tensor_total = lax.axis_size("tensor")
    rows = slot_count * seq_length
    if (
        tensor_total > 1
        and output_portion % 128 == 0
        and dim_shard % output_portion == 0
        and rows % (16 * CHUNKS) == 0
        and rank % 16 == 0
        and group_total > 1
        and full_out * dim_shard <= 1 << 22
    ):
        keep = selection.reshape(group_total * capacity, holder_count).astype(jnp.bfloat16)
        pick = pick_table.reshape(slot_count, group_total * capacity).astype(jnp.bfloat16)

        def widen(table):
            down, across = table.shape
            spot = jnp.arange(1, across + 1, dtype=jnp.float32)
            hit = jnp.sum(table.astype(jnp.float32) * spot, axis=1).astype(jnp.int32) - 1
            target = hit[:, None] * rank + jnp.arange(rank, dtype=jnp.int32)
            target = jnp.where(hit[:, None] < 0, -1, target).reshape(down * rank)
            spots = jnp.arange(across * rank, dtype=jnp.int32)
            return (target[:, None] == spots[None, :]).astype(jnp.bfloat16)

        keep_wide = widen(keep)

        def stored(came):
            rows_of = lax.dot_general(
                keep_wide, came, (((0,), (0,)), ((), ())), preferred_element_type=jnp.float32
            )
            return rows_of.reshape(holder_count, rank, came.shape[1])

        alive = (slot_ids < group_live_counts[0]).astype(jnp.float32)
        alive = jnp.broadcast_to(alive[:, None], (slot_count, 128))
        key_value, grad_in, down_part, up_part = line_call(
            tensor_total,
            group_total,
            slot_count,
            activations.reshape(rows, dim_shard),
            frozen_weight,
            cotangent.reshape(rows, output_portion),
            alive,
            adapter_down_weight.reshape(holder_count * rank, dim_shard),
            adapter_up_weight.reshape(holder_count * rank, output_portion),
            keep_wide,
            widen(pick),
        )
        return (
            key_value.reshape(slot_count, seq_length, output_portion),
            grad_in.reshape(slot_count, seq_length, dim_shard),
            stored(down_part),
            stored(up_part),
        )
    every_down, every_up = (
        lax.all_gather(adapter_down_weight, "dp", axis=0, tiled=True),
        lax.all_gather(adapter_up_weight, "dp", axis=0, tiled=True),
    )
    mine_rows = lax.dynamic_slice_in_dim(adapter_rows, group_index * slot_count, slot_count)
    one_hot = (
        mine_rows[:, None] == jnp.arange(group_total * holder_count, dtype=jnp.int32)[None, :]
    ).astype(jnp.bfloat16)
    down_weight_slice = jnp.einsum(
        "ja,ard->jrd", one_hot, every_down, preferred_element_type=jnp.float32
    ).astype(jnp.bfloat16)
    up_weight_slice = jnp.einsum(
        "ja,arw->jrw", one_hot, every_up, preferred_element_type=jnp.float32
    ).astype(jnp.bfloat16)
    low_sum = lax.psum(
        jnp.einsum(
            "cfy,cjy->cfj", activations, down_weight_slice, preferred_element_type=jnp.float32
        ).astype(jnp.bfloat16),
        "tensor",
    )
    partial_value = jnp.dot(
        activations.reshape(slot_count * seq_length, dim_shard),
        frozen_weight,
        preferred_element_type=jnp.float32,
    ).reshape(slot_count, seq_length, full_out)
    whole_sum = lax.psum(partial_value.astype(jnp.bfloat16), "tensor").astype(jnp.float32)
    frozen_output = lax.dynamic_slice_in_dim(
        whole_sum, tensor_index * output_portion, output_portion, 2
    )
    live_mask_float = live_sequence_mask.astype(jnp.float32)
    adapter_contribution = jnp.einsum(
        "slr,srw->slw", low_sum, up_weight_slice, preferred_element_type=jnp.float32
    )
    key_value_output = (
        (frozen_output + adapter_scale * adapter_contribution) * live_mask_float
    ).astype(jnp.bfloat16)
    masked = cotangent * live_sequence_mask
    masked_full = lax.all_gather(masked, "tensor", axis=2, tiled=True)
    back_sum = lax.psum(
        (
            adapter_scale
            * jnp.einsum(
                "bvg,bqg->bvq", masked, up_weight_slice, preferred_element_type=jnp.float32
            )
        ).astype(jnp.bfloat16),
        "tensor",
    )
    frozen_path = lax.dot_general(
        masked_full.reshape(slot_count * seq_length, full_out),
        frozen_weight,
        (((1,), (1,)), ((), ())),
        preferred_element_type=jnp.float32,
    )
    input_gradient = frozen_path.reshape(slot_count, seq_length, dim_shard) + jnp.einsum(
        "qip,qpb->qib", back_sum, down_weight_slice, preferred_element_type=jnp.float32
    )
    grad_input = (input_gradient * live_mask_float).astype(jnp.bfloat16)
    down_contributions = jnp.einsum(
        "ihn,ihx->inx", back_sum, activations, preferred_element_type=jnp.float32
    )
    up_contributions = adapter_scale * jnp.einsum(
        "tun,tuq->tnq", low_sum, masked, preferred_element_type=jnp.float32
    )
    send_grad_down = jnp.einsum(
        "joc,jrd->ocrd", pick_table, down_contributions, precision=lax.Precision.HIGHEST
    )
    send_grad_up = jnp.einsum(
        "joc,jrw->ocrw", pick_table, up_contributions, precision=lax.Precision.HIGHEST
    )
    back_down, back_up = (
        lax.all_to_all(
            send_grad_down.astype(jnp.bfloat16), "dp", split_axis=0, concat_axis=0, tiled=True
        ).astype(send_grad_down.dtype),
        lax.all_to_all(
            send_grad_up.astype(jnp.bfloat16), "dp", split_axis=0, concat_axis=0, tiled=True
        ).astype(send_grad_up.dtype),
    )
    grad_down = jnp.einsum("eck,ecrd->krd", selection, back_down, precision=lax.Precision.HIGHEST)
    grad_up = jnp.einsum("eck,ecrw->krw", selection, back_up, precision=lax.Precision.HIGHEST)
    return (key_value_output, grad_input, grad_down, grad_up)


def solution(mesh):
    in_specs = (
        P(("parts", "dp"), None, "tensor"),
        P("tensor", None),
        P(("parts", "dp"), None, "tensor"),
        P(("parts", "dp"), None, "tensor"),
        P(("parts", "dp"), None, "tensor"),
        P("parts"),
        P("parts"),
        P(("parts", "dp")),
    )
    out_specs = (
        P(("parts", "dp"), None, "tensor"),
        P(("parts", "dp"), None, "tensor"),
        P(("parts", "dp"), None, "tensor"),
        P(("parts", "dp"), None, "tensor"),
    )
    return jax.shard_map(shards, mesh=mesh, in_specs=in_specs, out_specs=out_specs, check_vma=False)
```

```python
import functools

import jax
import jax.numpy as jnp
from jax import lax
from jax.experimental import pallas as pl
from jax.experimental.pallas import tpu as pltpu
from jax.sharding import PartitionSpec as P

CAP_OWN = 2


adapter_scale = 2.0


CHUNKS = 4
MESH = pl.DeviceIdType.MESH
NT = (((1,), (1,)), ((), ()))
TN = (((0,), (0,)), ((), ()))


def line_kernel(
    n, groups, chunks, slots,
    x_hbm, w_hbm, cot_ref, live_ref, store_down, store_up, keep_ref, pick_ref,
    kv_ref, gin_hbm, back_ref, up_back_ref,
    alive_ref, panels, asked, came, given, landed, dp_send, dp_recv,
    x_ref, w_ref, full, part, from_left, from_right, acc, small, lowt, backt,
    load_sem, ag_recv, ag_right, ag_left, rs_recv_r, rs_recv_l, rs_send_r, rs_send_l,
    small_send, small_recv,
):
    me = lax.axis_index("tensor")
    rows, width = cot_ref.shape
    depth = x_ref.shape[1]
    rank = small.shape[1] // 2
    size = rows // chunks
    length = rows // slots
    last = n - 1
    mirror = last - me

    def chunk(c):
        return pl.ds(pl.multiple_of(c * size, size), size)

    def columns(d):
        return pl.ds(pl.multiple_of(d * width, width), width)

    def ag_copy(b, c, to_right):
        return pltpu.make_async_remote_copy(
            src_ref=full.at[b, chunk(c)],
            dst_ref=full.at[b, chunk(c)],
            send_sem=(ag_right if to_right else ag_left).at[b, c],
            recv_sem=ag_recv.at[b, c],
            device_id={"tensor": me + 1 if to_right else me - 1},
            device_id_type=MESH,
        )

    def rs_copy(d, c, to_right):
        return pltpu.make_async_remote_copy(
            src_ref=part.at[d, chunk(c)],
            dst_ref=(from_left if to_right else from_right).at[d, chunk(c)],
            send_sem=(rs_send_r if to_right else rs_send_l).at[d, c],
            recv_sem=(rs_recv_r if to_right else rs_recv_l).at[d, c],
            device_id={"tensor": me + 1 if to_right else me - 1},
            device_id_type=MESH,
        )

    def small_copy(peer, slot):
        return pltpu.make_async_remote_copy(
            src_ref=small.at[slot],
            dst_ref=small.at[slot],
            send_sem=small_send.at[peer],
            recv_sem=small_recv.at[slot],
            device_id={"tensor": peer},
            device_id_type=MESH,
        )

    group = lax.axis_index("dp")
    share = asked.shape[1]
    parts = depth // width
    down_ref = panels.at[:, pl.ds(0, depth)]
    up_ref = panels.at[:, pl.ds(depth, width)]

    def dp_copy(step, way, receiving):
        peer = lax.rem(group + step, groups)
        source, target = ((asked, came), (given, landed))[way]
        slot = peer if receiving else group
        return pltpu.make_async_remote_copy(
            src_ref=source.at[peer],
            dst_ref=target.at[slot],
            send_sem=dp_send.at[way, peer],
            recv_sem=dp_recv.at[way, slot],
            device_id={"dp": peer},
            device_id_type=MESH,
        )

    load_x = pltpu.make_async_copy(x_hbm, x_ref, load_sem.at[0])
    load_w = pltpu.make_async_copy(w_hbm, w_ref, load_sem.at[1])
    load_x.start()
    load_w.start()
    barrier = pltpu.get_barrier_semaphore()
    for step in range(1, n):
        pl.semaphore_signal(
            barrier, inc=1, device_id={"tensor": lax.rem(me + step, n)}, device_id_type=MESH
        )
    for step in range(1, groups):
        pl.semaphore_signal(
            barrier, inc=1, device_id={"dp": lax.rem(group + step, groups)}, device_id_type=MESH
        )
    alive_ref[...] = jnp.concatenate(
        [jnp.broadcast_to(live_ref[s : s + 1, :1], (length, 1)) for s in range(slots)], axis=0
    )
    full[me] = (cot_ref[...].astype(jnp.float32) * alive_ref[...]).astype(full.dtype)
    for j in range(parts + 1):
        if j < parts:
            store = store_down[:, j * width : (j + 1) * width]
        else:
            store = store_up[...]
        chosen = jnp.dot(
            keep_ref[...], store, preferred_element_type=jnp.float32
        ).astype(asked.dtype)
        for e in range(groups):
            asked[e, :, j * width : (j + 1) * width] = chosen[e * share : (e + 1) * share]
    pl.semaphore_wait(barrier, n + groups - 2)
    for step in range(1, groups):
        dp_copy(step, 0, False).start()
    came[group] = asked[group]


    def offer(low_chunk, high_chunk):
        @pl.loop(low_chunk, high_chunk)
        def _(c):
            @pl.when(me < last)
            def _():
                ag_copy(me, c, True).start()

            @pl.when(me > 0)
            def _():
                ag_copy(me, c, False).start()

    offer(0, chunks // 2)
    shape = (slots * rank, rows)
    slot_of_row = lax.broadcasted_iota(jnp.int32, shape, 0) // rank
    slot_of_column = lax.broadcasted_iota(jnp.int32, shape, 1) // length
    diagonal = slot_of_row == slot_of_column

    def compact(wide):
        wide = jnp.where(diagonal, wide, 0.0)
        total = wide[0:rank]
        for s in range(1, slots):
            total = total + wide[s * rank : (s + 1) * rank]
        return total

    for step in range(1, groups):
        dp_copy(step, 0, True).wait_recv()
    for j in range(parts + 1):
        block = came[:, :, j * width : (j + 1) * width].reshape(groups * share, width)
        panels[:, j * width : (j + 1) * width] = jnp.dot(
            pick_ref[...], block, preferred_element_type=jnp.float32
        ).astype(panels.dtype)
    back_part = compact(
        lax.dot_general(up_ref[...], full[me], NT, preferred_element_type=jnp.float32)
    )
    small[me, rank:, :] = (adapter_scale * back_part).astype(small.dtype)
    load_x.wait()
    low_part = compact(
        lax.dot_general(down_ref[...], x_ref[...], NT, preferred_element_type=jnp.float32)
    )
    small[me, :rank, :] = low_part.astype(small.dtype)
    for step in range(1, n):
        small_copy(lax.rem(me + step, n), me).start()

    offer(chunks // 2, chunks)
    load_w.wait()

    @pl.loop(0, n)
    def _(k):
        d = jnp.where(me == 0, last - k, k)

        @pl.loop(0, chunks)
        def _(c):
            part[d, chunk(c), :] = jnp.dot(
                x_ref[chunk(c), :], w_ref[:, columns(d)], preferred_element_type=jnp.float32
            ).astype(part.dtype)

            @pl.when((me == 0) & (d > 0))
            def _():
                rs_copy(d, c, True).start()

            @pl.when((me == last) & (d < last))
            def _():
                rs_copy(d, c, False).start()

    def frozen(b, first):
        @pl.loop(0, chunks)
        def _(c):
            @pl.loop(0, depth // width)
            def _(j):
                piece = lax.dot_general(
                    full[b, chunk(c), :],
                    w_ref[columns(j), columns(b)],
                    NT,
                    preferred_element_type=jnp.float32,
                )
                if first:
                    acc[chunk(c), columns(j)] = piece
                else:
                    acc[chunk(c), columns(j)] += piece

    def receive(q, c):
        @pl.when(q < me)
        def _():
            b = me - 1 - q
            ag_copy(b, c, True).wait_recv()

            @pl.when(me < last)
            def _():
                ag_copy(b, c, True).start()

        @pl.when((q >= me) & (me > 0))
        def _():
            d = last - (q - me)
            rs_copy(d, c, True).wait_recv()
            part[d, chunk(c), :] = (
                part[d, chunk(c), :].astype(jnp.float32)
                + from_left[d, chunk(c), :].astype(jnp.float32)
            ).astype(part.dtype)
            rs_copy(d, c, True).start()

        @pl.when(q < mirror)
        def _():
            b = me + 1 + q
            ag_copy(b, c, False).wait_recv()

            @pl.when(me > 0)
            def _():
                ag_copy(b, c, False).start()

        @pl.when((q >= mirror) & (me < last))
        def _():
            d = q - mirror
            rs_copy(d, c, False).wait_recv()
            part[d, chunk(c), :] = (
                part[d, chunk(c), :].astype(jnp.float32)
                + from_right[d, chunk(c), :].astype(jnp.float32)
            ).astype(part.dtype)
            rs_copy(d, c, False).start()

    def arrivals(q):
        @pl.loop(0, chunks)
        def _(c):
            receive(q, c)

    def products(q):
        @pl.when(q < me)
        def _():
            frozen(me - 1 - q, False)

        @pl.when(q < mirror)
        def _():
            frozen(me + 1 + q, False)

    arrivals(0)
    frozen(me, True)
    products(0)

    @pl.loop(1, last - 1)
    def _(q):
        arrivals(q)
        products(q)

    for step in range(1, n):
        source = lax.rem(me + step, n)
        small_copy(source, source).wait_recv()
    total = small[0].astype(jnp.float32)
    for b in range(1, n):
        total = total + small[b].astype(jnp.float32)
    low = jnp.where(diagonal, jnp.concatenate([total[:rank]] * slots, axis=0), 0.0)
    back = jnp.where(diagonal, jnp.concatenate([total[rank:]] * slots, axis=0), 0.0)
    lowt[...] = low.astype(lowt.dtype)
    backt[...] = back.astype(backt.dtype)
    for j in range(parts + 1):
        if j < parts:
            block = jnp.dot(
                backt[...],
                x_ref[:, j * width : (j + 1) * width],
                preferred_element_type=jnp.float32,
            )
        else:
            block = adapter_scale * jnp.dot(
                lowt[...], full[me], preferred_element_type=jnp.float32
            )
        block = lax.dot_general(
            pick_ref[...], block.astype(given.dtype), TN, preferred_element_type=jnp.float32
        ).astype(given.dtype)
        for e in range(groups):
            given[e, :, j * width : (j + 1) * width] = block[e * share : (e + 1) * share]
    for step in range(1, groups):
        dp_copy(step, 1, False).start()
    landed[group] = given[group]

    @pl.loop(max(last - 1, 1), last)
    def _(q):
        arrivals(q)
        products(q)

    @pl.loop(0, parts)
    def _(j):
        x_ref[:, columns(j)] = (
            alive_ref[...]
            * (
                acc[:, columns(j)]
                + lax.dot_general(
                    backt[...], panels[:, columns(j)], TN, preferred_element_type=jnp.float32
                )
            )
        ).astype(x_ref.dtype)

    store_x = pltpu.make_async_copy(x_ref, gin_hbm, load_sem.at[2])
    store_x.start()
    acc[:, :width] = adapter_scale * lax.dot_general(
        lowt[...], up_ref[...], TN, preferred_element_type=jnp.float32
    )

    def rs_finish(c, to_right):
        rs_copy(me, c, to_right).wait_recv()
        arrived = from_left if to_right else from_right
        acc[chunk(c), :width] += arrived[me, chunk(c), :].astype(jnp.float32)

    @pl.loop(0, chunks)
    def _(c):
        acc[chunk(c), :width] += part[me, chunk(c), :].astype(jnp.float32)

        @pl.when(me > 0)
        def _():
            rs_finish(c, True)

        @pl.when(me < last)
        def _():
            rs_finish(c, False)

        kv_ref[chunk(c), :] = (alive_ref[chunk(c), :] * acc[chunk(c), :width]).astype(kv_ref.dtype)

    for step in range(1, groups):
        dp_copy(step, 1, True).wait_recv()
    back_ref[...] = landed[:, :, :depth].reshape(back_ref.shape)
    up_back_ref[...] = landed[:, :, depth:].reshape(up_back_ref.shape)

    def drain(b, c):
        @pl.when((b <= me) & (me < last))
        def _():
            ag_copy(b, c, True).wait_send()

        @pl.when((b >= me) & (me > 0))
        def _():
            ag_copy(b, c, False).wait_send()

        @pl.when(b > me)
        def _():
            rs_copy(b, c, True).wait_send()

        @pl.when(b < me)
        def _():
            rs_copy(b, c, False).wait_send()

    for step in range(1, n):
        small_copy(lax.rem(me + step, n), me).wait_send()
    for step in range(1, groups):
        dp_copy(step, 0, False).wait_send()
        dp_copy(step, 1, False).wait_send()
    store_x.wait()

    @pl.loop(0, n)
    def _(b):
        @pl.loop(0, chunks)
        def _(c):
            drain(b, c)


def line_call(n, groups, slots, x, w, cot, alive, down, up, keep, pick):
    rows, depth = x.shape
    width = cot.shape[1]
    panel = pick.shape[0]
    rank = panel // slots
    share = keep.shape[0] // groups
    bf16 = jnp.bfloat16
    vmem = pl.BlockSpec(memory_space=pltpu.VMEM)
    hbm = pl.BlockSpec(memory_space=pl.ANY)
    dma = pltpu.SemaphoreType.DMA((n, CHUNKS))
    return pl.pallas_call(
        functools.partial(line_kernel, n, groups, CHUNKS, slots),
        out_shape=(
            jax.ShapeDtypeStruct((rows, width), bf16),
            jax.ShapeDtypeStruct((rows, depth), bf16),
            jax.ShapeDtypeStruct((keep.shape[0], depth), bf16),
            jax.ShapeDtypeStruct((keep.shape[0], width), bf16),
        ),
        in_specs=[hbm, hbm, vmem, vmem, vmem, vmem, vmem, vmem],
        out_specs=(vmem, hbm, vmem, vmem),
        scratch_shapes=[
            pltpu.VMEM((rows, 1), jnp.float32),
            pltpu.VMEM((panel, depth + width), bf16),
            pltpu.VMEM((groups, share, depth + width), bf16),
            pltpu.VMEM((groups, share, depth + width), bf16),
            pltpu.VMEM((groups, share, depth + width), bf16),
            pltpu.VMEM((groups, share, depth + width), bf16),
            pltpu.SemaphoreType.DMA((2, groups)),
            pltpu.SemaphoreType.DMA((2, groups)),
            pltpu.VMEM((rows, depth), bf16),
            pltpu.VMEM(w.shape, bf16),
            pltpu.VMEM((n, rows, width), bf16),
            pltpu.VMEM((n, rows, width), bf16),
            pltpu.VMEM((n, rows, width), bf16),
            pltpu.VMEM((n, rows, width), bf16),
            pltpu.VMEM((rows, depth), jnp.float32),
            pltpu.VMEM((n, 2 * rank, rows), bf16),
            pltpu.VMEM((panel, rows), bf16),
            pltpu.VMEM((panel, rows), bf16),
            pltpu.SemaphoreType.DMA((3,)),
            dma, dma, dma, dma, dma, dma, dma,
            pltpu.SemaphoreType.DMA((n,)),
            pltpu.SemaphoreType.DMA((n,)),
        ],
        compiler_params=pltpu.CompilerParams(
            collective_id=0, has_side_effects=True, vmem_limit_bytes=60 << 20
        ),
        cost_estimate=pl.CostEstimate(
            flops=4 * rows * depth * n * width, bytes_accessed=30_000_000, transcendentals=0
        ),
    )(x, w, cot, alive, down, up, keep, pick)


def shards(
    activations,
    frozen_weight,
    cotangent,
    adapter_down_weight,
    adapter_up_weight,
    sequence_adapter,
    adapter_store_row,
    group_live_counts,
):
    group_total = lax.axis_size("dp")
    slot_count, seq_length, dim_shard = activations.shape
    holder_count = adapter_down_weight.shape[0]
    output_portion = adapter_up_weight.shape[2]
    full_out = frozen_weight.shape[1]
    group_index = lax.axis_index("dp")
    tensor_index = lax.axis_index("tensor")
    capacity = CAP_OWN
    adapter_rows = adapter_store_row[sequence_adapter]
    owners = (adapter_rows // holder_count).reshape(group_total, slot_count)
    local_rows = (adapter_rows % holder_count).reshape(group_total, slot_count)
    slot_ids = jnp.arange(slot_count, dtype=jnp.int32)
    same_owner = owners[:, :, None] == owners[:, None, :]
    earlier_slot = slot_ids[None, :] < slot_ids[:, None]
    owner_rank = jnp.sum((same_owner & earlier_slot[None]).astype(jnp.int32), axis=2)
    cap_ids = jnp.arange(capacity, dtype=jnp.int32)
    owner_hits = (
        (owners == group_index)[:, :, None] & (owner_rank[:, :, None] == cap_ids[None, None, :])
    ).astype(jnp.float32)
    local_match = (
        local_rows[:, :, None] == jnp.arange(holder_count, dtype=jnp.int32)[None, None, :]
    ).astype(jnp.float32)
    selection = jnp.einsum("ejc,ejk->eck", owner_hits, local_match)
    mine_owner = lax.dynamic_index_in_dim(owners, group_index, 0, keepdims=False)
    mine_rank = lax.dynamic_index_in_dim(owner_rank, group_index, 0, keepdims=False)
    group_ids = jnp.arange(group_total, dtype=jnp.int32)
    pick_table = (
        (mine_owner[:, None] == group_ids[None, :])[:, :, None]
        & (mine_rank[:, None] == cap_ids[None, :])[:, None, :]
    ).astype(jnp.float32)
    live_sequence_mask = (slot_ids < group_live_counts[0]).astype(jnp.bfloat16)[:, None, None]
    rank = adapter_down_weight.shape[1]
    tensor_total = lax.axis_size("tensor")
    rows = slot_count * seq_length
    if (
        tensor_total > 1
        and output_portion % 128 == 0
        and dim_shard % output_portion == 0
        and rows % (16 * CHUNKS) == 0
        and rank % 16 == 0
        and group_total > 1
        and full_out * dim_shard <= 1 << 22
    ):
        keep = selection.reshape(group_total * capacity, holder_count).astype(jnp.bfloat16)
        pick = pick_table.reshape(slot_count, group_total * capacity).astype(jnp.bfloat16)

        def widen(table):
            down, across = table.shape
            spot = jnp.arange(1, across + 1, dtype=jnp.float32)
            hit = jnp.sum(table.astype(jnp.float32) * spot, axis=1).astype(jnp.int32) - 1
            target = hit[:, None] * rank + jnp.arange(rank, dtype=jnp.int32)
            target = jnp.where(hit[:, None] < 0, -1, target).reshape(down * rank)
            spots = jnp.arange(across * rank, dtype=jnp.int32)
            return (target[:, None] == spots[None, :]).astype(jnp.bfloat16)

        keep_wide = widen(keep)

        def stored(came):
            rows_of = lax.dot_general(
                keep_wide, came, (((0,), (0,)), ((), ())), preferred_element_type=jnp.float32
            )
            return rows_of.reshape(holder_count, rank, came.shape[1])

        alive = (slot_ids < group_live_counts[0]).astype(jnp.float32)
        alive = jnp.broadcast_to(alive[:, None], (slot_count, 128))
        key_value, grad_in, down_part, up_part = line_call(
            tensor_total,
            group_total,
            slot_count,
            activations.reshape(rows, dim_shard),
            frozen_weight,
            cotangent.reshape(rows, output_portion),
            alive,
            adapter_down_weight.reshape(holder_count * rank, dim_shard),
            adapter_up_weight.reshape(holder_count * rank, output_portion),
            keep_wide,
            widen(pick),
        )
        return (
            key_value.reshape(slot_count, seq_length, output_portion),
            grad_in.reshape(slot_count, seq_length, dim_shard),
            stored(down_part),
            stored(up_part),
        )
    every_down, every_up = (
        lax.all_gather(adapter_down_weight, "dp", axis=0, tiled=True),
        lax.all_gather(adapter_up_weight, "dp", axis=0, tiled=True),
    )
    mine_rows = lax.dynamic_slice_in_dim(adapter_rows, group_index * slot_count, slot_count)
    one_hot = (
        mine_rows[:, None] == jnp.arange(group_total * holder_count, dtype=jnp.int32)[None, :]
    ).astype(jnp.bfloat16)
    down_weight_slice = jnp.einsum(
        "ja,ard->jrd", one_hot, every_down, preferred_element_type=jnp.float32
    ).astype(jnp.bfloat16)
    up_weight_slice = jnp.einsum(
        "ja,arw->jrw", one_hot, every_up, preferred_element_type=jnp.float32
    ).astype(jnp.bfloat16)
    low_sum = lax.psum(
        jnp.einsum(
            "cfy,cjy->cfj", activations, down_weight_slice, preferred_element_type=jnp.float32
        ).astype(jnp.bfloat16),
        "tensor",
    )
    partial_value = jnp.dot(
        activations.reshape(slot_count * seq_length, dim_shard),
        frozen_weight,
        preferred_element_type=jnp.float32,
    ).reshape(slot_count, seq_length, full_out)
    whole_sum = lax.psum(partial_value.astype(jnp.bfloat16), "tensor").astype(jnp.float32)
    frozen_output = lax.dynamic_slice_in_dim(
        whole_sum, tensor_index * output_portion, output_portion, 2
    )
    live_mask_float = live_sequence_mask.astype(jnp.float32)
    adapter_contribution = jnp.einsum(
        "slr,srw->slw", low_sum, up_weight_slice, preferred_element_type=jnp.float32
    )
    key_value_output = (
        (frozen_output + adapter_scale * adapter_contribution) * live_mask_float
    ).astype(jnp.bfloat16)
    masked = cotangent * live_sequence_mask
    masked_full = lax.all_gather(masked, "tensor", axis=2, tiled=True)
    back_sum = lax.psum(
        (
            adapter_scale
            * jnp.einsum(
                "bvg,bqg->bvq", masked, up_weight_slice, preferred_element_type=jnp.float32
            )
        ).astype(jnp.bfloat16),
        "tensor",
    )
    frozen_path = lax.dot_general(
        masked_full.reshape(slot_count * seq_length, full_out),
        frozen_weight,
        (((1,), (1,)), ((), ())),
        preferred_element_type=jnp.float32,
    )
    input_gradient = frozen_path.reshape(slot_count, seq_length, dim_shard) + jnp.einsum(
        "qip,qpb->qib", back_sum, down_weight_slice, preferred_element_type=jnp.float32
    )
    grad_input = (input_gradient * live_mask_float).astype(jnp.bfloat16)
    down_contributions = jnp.einsum(
        "ihn,ihx->inx", back_sum, activations, preferred_element_type=jnp.float32
    )
    up_contributions = adapter_scale * jnp.einsum(
        "tun,tuq->tnq", low_sum, masked, preferred_element_type=jnp.float32
    )
    send_grad_down = jnp.einsum(
        "joc,jrd->ocrd", pick_table, down_contributions, precision=lax.Precision.HIGHEST
    )
    send_grad_up = jnp.einsum(
        "joc,jrw->ocrw", pick_table, up_contributions, precision=lax.Precision.HIGHEST
    )
    back_down, back_up = (
        lax.all_to_all(
            send_grad_down.astype(jnp.bfloat16), "dp", split_axis=0, concat_axis=0, tiled=True
        ).astype(send_grad_down.dtype),
        lax.all_to_all(
            send_grad_up.astype(jnp.bfloat16), "dp", split_axis=0, concat_axis=0, tiled=True
        ).astype(send_grad_up.dtype),
    )
    grad_down = jnp.einsum("eck,ecrd->krd", selection, back_down, precision=lax.Precision.HIGHEST)
    grad_up = jnp.einsum("eck,ecrw->krw", selection, back_up, precision=lax.Precision.HIGHEST)
    return (key_value_output, grad_input, grad_down, grad_up)


def solution(mesh):
    in_specs = (
        P(("parts", "dp"), None, "tensor"),
        P("tensor", None),
        P(("parts", "dp"), None, "tensor"),
        P(("parts", "dp"), None, "tensor"),
        P(("parts", "dp"), None, "tensor"),
        P("parts"),
        P("parts"),
        P(("parts", "dp")),
    )
    out_specs = (
        P(("parts", "dp"), None, "tensor"),
        P(("parts", "dp"), None, "tensor"),
        P(("parts", "dp"), None, "tensor"),
        P(("parts", "dp"), None, "tensor"),
    )
    return jax.shard_map(shards, mesh=mesh, in_specs=in_specs, out_specs=out_specs, check_vma=False)
```

```python
import functools

import jax
import jax.numpy as jnp
from jax import lax
from jax.experimental import pallas as pl
from jax.experimental.pallas import tpu as pltpu
from jax.sharding import PartitionSpec as P

CAP_OWN = 2


adapter_scale = 2.0


CHUNKS = 5
MESH = pl.DeviceIdType.MESH
NT = (((1,), (1,)), ((), ()))
TN = (((0,), (0,)), ((), ()))


def line_kernel(
    n, groups, chunks, slots,
    x_hbm, w_hbm, cot_ref, live_ref, store_down, store_up, keep_ref, pick_ref,
    kv_ref, gin_hbm, back_ref, up_back_ref,
    alive_ref, panels, asked, came, given, landed, dp_send, dp_recv,
    x_ref, w_ref, full, part, from_left, from_right, acc, small, lowt, backt,
    load_sem, ag_recv, ag_right, ag_left, rs_recv_r, rs_recv_l, rs_send_r, rs_send_l,
    small_send, small_recv,
):
    me = lax.axis_index("tensor")
    rows, width = cot_ref.shape
    depth = x_ref.shape[1]
    rank = small.shape[1] // 2
    size = rows // chunks
    length = rows // slots
    last = n - 1
    mirror = last - me

    def chunk(c):
        return pl.ds(pl.multiple_of(c * size, size), size)

    def columns(d):
        return pl.ds(pl.multiple_of(d * width, width), width)

    def ag_copy(b, c, to_right):
        return pltpu.make_async_remote_copy(
            src_ref=full.at[b, chunk(c)],
            dst_ref=full.at[b, chunk(c)],
            send_sem=(ag_right if to_right else ag_left).at[b, c],
            recv_sem=ag_recv.at[b, c],
            device_id={"tensor": me + 1 if to_right else me - 1},
            device_id_type=MESH,
        )

    def rs_copy(d, c, to_right):
        return pltpu.make_async_remote_copy(
            src_ref=part.at[d, chunk(c)],
            dst_ref=(from_left if to_right else from_right).at[d, chunk(c)],
            send_sem=(rs_send_r if to_right else rs_send_l).at[d, c],
            recv_sem=(rs_recv_r if to_right else rs_recv_l).at[d, c],
            device_id={"tensor": me + 1 if to_right else me - 1},
            device_id_type=MESH,
        )

    def small_copy(peer, slot):
        return pltpu.make_async_remote_copy(
            src_ref=small.at[slot],
            dst_ref=small.at[slot],
            send_sem=small_send.at[peer],
            recv_sem=small_recv.at[slot],
            device_id={"tensor": peer},
            device_id_type=MESH,
        )

    group = lax.axis_index("dp")
    share = asked.shape[1]
    parts = depth // width
    down_ref = panels.at[:, pl.ds(0, depth)]
    up_ref = panels.at[:, pl.ds(depth, width)]

    def dp_copy(step, way, receiving):
        peer = lax.rem(group + step, groups)
        source, target = ((asked, came), (given, landed))[way]
        slot = peer if receiving else group
        return pltpu.make_async_remote_copy(
            src_ref=source.at[peer],
            dst_ref=target.at[slot],
            send_sem=dp_send.at[way, peer],
            recv_sem=dp_recv.at[way, slot],
            device_id={"dp": peer},
            device_id_type=MESH,
        )

    load_x = pltpu.make_async_copy(x_hbm, x_ref, load_sem.at[0])
    load_w = pltpu.make_async_copy(w_hbm, w_ref, load_sem.at[1])
    load_x.start()
    load_w.start()
    barrier = pltpu.get_barrier_semaphore()
    for step in range(1, n):
        pl.semaphore_signal(
            barrier, inc=1, device_id={"tensor": lax.rem(me + step, n)}, device_id_type=MESH
        )
    for step in range(1, groups):
        pl.semaphore_signal(
            barrier, inc=1, device_id={"dp": lax.rem(group + step, groups)}, device_id_type=MESH
        )
    alive_ref[...] = jnp.concatenate(
        [jnp.broadcast_to(live_ref[s : s + 1, :1], (length, 1)) for s in range(slots)], axis=0
    )
    full[me] = (cot_ref[...].astype(jnp.float32) * alive_ref[...]).astype(full.dtype)
    for j in range(parts + 1):
        if j < parts:
            store = store_down[:, j * width : (j + 1) * width]
        else:
            store = store_up[...]
        chosen = jnp.dot(
            keep_ref[...], store, preferred_element_type=jnp.float32
        ).astype(asked.dtype)
        for e in range(groups):
            asked[e, :, j * width : (j + 1) * width] = chosen[e * share : (e + 1) * share]
    pl.semaphore_wait(barrier, n + groups - 2)
    for step in range(1, groups):
        dp_copy(step, 0, False).start()
    came[group] = asked[group]


    def offer(low_chunk, high_chunk):
        @pl.loop(low_chunk, high_chunk)
        def _(c):
            @pl.when(me < last)
            def _():
                ag_copy(me, c, True).start()

            @pl.when(me > 0)
            def _():
                ag_copy(me, c, False).start()

    offer(0, chunks // 2)
    shape = (slots * rank, rows)
    slot_of_row = lax.broadcasted_iota(jnp.int32, shape, 0) // rank
    slot_of_column = lax.broadcasted_iota(jnp.int32, shape, 1) // length
    diagonal = slot_of_row == slot_of_column

    def compact(wide):
        wide = jnp.where(diagonal, wide, 0.0)
        total = wide[0:rank]
        for s in range(1, slots):
            total = total + wide[s * rank : (s + 1) * rank]
        return total

    for step in range(1, groups):
        dp_copy(step, 0, True).wait_recv()
    for j in range(parts + 1):
        block = came[:, :, j * width : (j + 1) * width].reshape(groups * share, width)
        panels[:, j * width : (j + 1) * width] = jnp.dot(
            pick_ref[...], block, preferred_element_type=jnp.float32
        ).astype(panels.dtype)
    back_part = compact(
        lax.dot_general(up_ref[...], full[me], NT, preferred_element_type=jnp.float32)
    )
    small[me, rank:, :] = (adapter_scale * back_part).astype(small.dtype)
    load_x.wait()
    low_part = compact(
        lax.dot_general(down_ref[...], x_ref[...], NT, preferred_element_type=jnp.float32)
    )
    small[me, :rank, :] = low_part.astype(small.dtype)
    for step in range(1, n):
        small_copy(lax.rem(me + step, n), me).start()

    offer(chunks // 2, chunks)
    load_w.wait()

    @pl.loop(0, n)
    def _(k):
        d = jnp.where(me == 0, last - k, k)

        @pl.loop(0, chunks)
        def _(c):
            part[d, chunk(c), :] = jnp.dot(
                x_ref[chunk(c), :], w_ref[:, columns(d)], preferred_element_type=jnp.float32
            ).astype(part.dtype)

            @pl.when((me == 0) & (d > 0))
            def _():
                rs_copy(d, c, True).start()

            @pl.when((me == last) & (d < last))
            def _():
                rs_copy(d, c, False).start()

    def frozen(b, first):
        @pl.loop(0, chunks)
        def _(c):
            @pl.loop(0, depth // width)
            def _(j):
                piece = lax.dot_general(
                    full[b, chunk(c), :],
                    w_ref[columns(j), columns(b)],
                    NT,
                    preferred_element_type=jnp.float32,
                )
                if first:
                    acc[chunk(c), columns(j)] = piece
                else:
                    acc[chunk(c), columns(j)] += piece

    def receive(q, c):
        @pl.when(q < me)
        def _():
            b = me - 1 - q
            ag_copy(b, c, True).wait_recv()

            @pl.when(me < last)
            def _():
                ag_copy(b, c, True).start()

        @pl.when((q >= me) & (me > 0))
        def _():
            d = last - (q - me)
            rs_copy(d, c, True).wait_recv()
            part[d, chunk(c), :] = (
                part[d, chunk(c), :].astype(jnp.float32)
                + from_left[d, chunk(c), :].astype(jnp.float32)
            ).astype(part.dtype)
            rs_copy(d, c, True).start()

        @pl.when(q < mirror)
        def _():
            b = me + 1 + q
            ag_copy(b, c, False).wait_recv()

            @pl.when(me > 0)
            def _():
                ag_copy(b, c, False).start()

        @pl.when((q >= mirror) & (me < last))
        def _():
            d = q - mirror
            rs_copy(d, c, False).wait_recv()
            part[d, chunk(c), :] = (
                part[d, chunk(c), :].astype(jnp.float32)
                + from_right[d, chunk(c), :].astype(jnp.float32)
            ).astype(part.dtype)
            rs_copy(d, c, False).start()

    def arrivals(q):
        @pl.loop(0, chunks)
        def _(c):
            receive(q, c)

    def products(q):
        @pl.when(q < me)
        def _():
            frozen(me - 1 - q, False)

        @pl.when(q < mirror)
        def _():
            frozen(me + 1 + q, False)

    arrivals(0)
    frozen(me, True)
    products(0)

    @pl.loop(1, last - 1)
    def _(q):
        arrivals(q)
        products(q)

    for step in range(1, n):
        source = lax.rem(me + step, n)
        small_copy(source, source).wait_recv()
    total = small[0].astype(jnp.float32)
    for b in range(1, n):
        total = total + small[b].astype(jnp.float32)
    low = jnp.where(diagonal, jnp.concatenate([total[:rank]] * slots, axis=0), 0.0)
    back = jnp.where(diagonal, jnp.concatenate([total[rank:]] * slots, axis=0), 0.0)
    lowt[...] = low.astype(lowt.dtype)
    backt[...] = back.astype(backt.dtype)
    for j in range(parts + 1):
        if j < parts:
            block = jnp.dot(
                backt[...],
                x_ref[:, j * width : (j + 1) * width],
                preferred_element_type=jnp.float32,
            )
        else:
            block = adapter_scale * jnp.dot(
                lowt[...], full[me], preferred_element_type=jnp.float32
            )
        block = lax.dot_general(
            pick_ref[...], block.astype(given.dtype), TN, preferred_element_type=jnp.float32
        ).astype(given.dtype)
        for e in range(groups):
            given[e, :, j * width : (j + 1) * width] = block[e * share : (e + 1) * share]
    for step in range(1, groups):
        dp_copy(step, 1, False).start()
    landed[group] = given[group]

    @pl.loop(max(last - 1, 1), last)
    def _(q):
        arrivals(q)
        products(q)

    @pl.loop(0, parts)
    def _(j):
        x_ref[:, columns(j)] = (
            alive_ref[...]
            * (
                acc[:, columns(j)]
                + lax.dot_general(
                    backt[...], panels[:, columns(j)], TN, preferred_element_type=jnp.float32
                )
            )
        ).astype(x_ref.dtype)

    store_x = pltpu.make_async_copy(x_ref, gin_hbm, load_sem.at[2])
    store_x.start()
    acc[:, :width] = adapter_scale * lax.dot_general(
        lowt[...], up_ref[...], TN, preferred_element_type=jnp.float32
    )

    def rs_finish(c, to_right):
        rs_copy(me, c, to_right).wait_recv()
        arrived = from_left if to_right else from_right
        acc[chunk(c), :width] += arrived[me, chunk(c), :].astype(jnp.float32)

    @pl.loop(0, chunks)
    def _(c):
        acc[chunk(c), :width] += part[me, chunk(c), :].astype(jnp.float32)

        @pl.when(me > 0)
        def _():
            rs_finish(c, True)

        @pl.when(me < last)
        def _():
            rs_finish(c, False)

        kv_ref[chunk(c), :] = (alive_ref[chunk(c), :] * acc[chunk(c), :width]).astype(kv_ref.dtype)

    for step in range(1, groups):
        dp_copy(step, 1, True).wait_recv()
    back_ref[...] = landed[:, :, :depth].reshape(back_ref.shape)
    up_back_ref[...] = landed[:, :, depth:].reshape(up_back_ref.shape)

    def drain(b, c):
        @pl.when((b <= me) & (me < last))
        def _():
            ag_copy(b, c, True).wait_send()

        @pl.when((b >= me) & (me > 0))
        def _():
            ag_copy(b, c, False).wait_send()

        @pl.when(b > me)
        def _():
            rs_copy(b, c, True).wait_send()

        @pl.when(b < me)
        def _():
            rs_copy(b, c, False).wait_send()

    for step in range(1, n):
        small_copy(lax.rem(me + step, n), me).wait_send()
    for step in range(1, groups):
        dp_copy(step, 0, False).wait_send()
        dp_copy(step, 1, False).wait_send()
    store_x.wait()

    @pl.loop(0, n)
    def _(b):
        @pl.loop(0, chunks)
        def _(c):
            drain(b, c)


def line_call(n, groups, slots, x, w, cot, alive, down, up, keep, pick):
    rows, depth = x.shape
    width = cot.shape[1]
    panel = pick.shape[0]
    rank = panel // slots
    share = keep.shape[0] // groups
    bf16 = jnp.bfloat16
    vmem = pl.BlockSpec(memory_space=pltpu.VMEM)
    hbm = pl.BlockSpec(memory_space=pl.ANY)
    dma = pltpu.SemaphoreType.DMA((n, CHUNKS))
    return pl.pallas_call(
        functools.partial(line_kernel, n, groups, CHUNKS, slots),
        out_shape=(
            jax.ShapeDtypeStruct((rows, width), bf16),
            jax.ShapeDtypeStruct((rows, depth), bf16),
            jax.ShapeDtypeStruct((keep.shape[0], depth), bf16),
            jax.ShapeDtypeStruct((keep.shape[0], width), bf16),
        ),
        in_specs=[hbm, hbm, vmem, vmem, vmem, vmem, vmem, vmem],
        out_specs=(vmem, hbm, vmem, vmem),
        scratch_shapes=[
            pltpu.VMEM((rows, 1), jnp.float32),
            pltpu.VMEM((panel, depth + width), bf16),
            pltpu.VMEM((groups, share, depth + width), bf16),
            pltpu.VMEM((groups, share, depth + width), bf16),
            pltpu.VMEM((groups, share, depth + width), bf16),
            pltpu.VMEM((groups, share, depth + width), bf16),
            pltpu.SemaphoreType.DMA((2, groups)),
            pltpu.SemaphoreType.DMA((2, groups)),
            pltpu.VMEM((rows, depth), bf16),
            pltpu.VMEM(w.shape, bf16),
            pltpu.VMEM((n, rows, width), bf16),
            pltpu.VMEM((n, rows, width), bf16),
            pltpu.VMEM((n, rows, width), bf16),
            pltpu.VMEM((n, rows, width), bf16),
            pltpu.VMEM((rows, depth), jnp.float32),
            pltpu.VMEM((n, 2 * rank, rows), bf16),
            pltpu.VMEM((panel, rows), bf16),
            pltpu.VMEM((panel, rows), bf16),
            pltpu.SemaphoreType.DMA((3,)),
            dma, dma, dma, dma, dma, dma, dma,
            pltpu.SemaphoreType.DMA((n,)),
            pltpu.SemaphoreType.DMA((n,)),
        ],
        compiler_params=pltpu.CompilerParams(
            collective_id=0, has_side_effects=True, vmem_limit_bytes=60 << 20
        ),
        cost_estimate=pl.CostEstimate(
            flops=4 * rows * depth * n * width, bytes_accessed=30_000_000, transcendentals=0
        ),
    )(x, w, cot, alive, down, up, keep, pick)


def shards(
    activations,
    frozen_weight,
    cotangent,
    adapter_down_weight,
    adapter_up_weight,
    sequence_adapter,
    adapter_store_row,
    group_live_counts,
):
    group_total = lax.axis_size("dp")
    slot_count, seq_length, dim_shard = activations.shape
    holder_count = adapter_down_weight.shape[0]
    output_portion = adapter_up_weight.shape[2]
    full_out = frozen_weight.shape[1]
    group_index = lax.axis_index("dp")
    tensor_index = lax.axis_index("tensor")
    capacity = CAP_OWN
    adapter_rows = adapter_store_row[sequence_adapter]
    owners = (adapter_rows // holder_count).reshape(group_total, slot_count)
    local_rows = (adapter_rows % holder_count).reshape(group_total, slot_count)
    slot_ids = jnp.arange(slot_count, dtype=jnp.int32)
    same_owner = owners[:, :, None] == owners[:, None, :]
    earlier_slot = slot_ids[None, :] < slot_ids[:, None]
    owner_rank = jnp.sum((same_owner & earlier_slot[None]).astype(jnp.int32), axis=2)
    cap_ids = jnp.arange(capacity, dtype=jnp.int32)
    owner_hits = (
        (owners == group_index)[:, :, None] & (owner_rank[:, :, None] == cap_ids[None, None, :])
    ).astype(jnp.float32)
    local_match = (
        local_rows[:, :, None] == jnp.arange(holder_count, dtype=jnp.int32)[None, None, :]
    ).astype(jnp.float32)
    selection = jnp.einsum("ejc,ejk->eck", owner_hits, local_match)
    mine_owner = lax.dynamic_index_in_dim(owners, group_index, 0, keepdims=False)
    mine_rank = lax.dynamic_index_in_dim(owner_rank, group_index, 0, keepdims=False)
    group_ids = jnp.arange(group_total, dtype=jnp.int32)
    pick_table = (
        (mine_owner[:, None] == group_ids[None, :])[:, :, None]
        & (mine_rank[:, None] == cap_ids[None, :])[:, None, :]
    ).astype(jnp.float32)
    live_sequence_mask = (slot_ids < group_live_counts[0]).astype(jnp.bfloat16)[:, None, None]
    rank = adapter_down_weight.shape[1]
    tensor_total = lax.axis_size("tensor")
    rows = slot_count * seq_length
    if (
        tensor_total > 1
        and output_portion % 128 == 0
        and dim_shard % output_portion == 0
        and rows % (16 * CHUNKS) == 0
        and rank % 16 == 0
        and group_total > 1
        and full_out * dim_shard <= 1 << 22
    ):
        keep = selection.reshape(group_total * capacity, holder_count).astype(jnp.bfloat16)
        pick = pick_table.reshape(slot_count, group_total * capacity).astype(jnp.bfloat16)

        def widen(table):
            down, across = table.shape
            spot = jnp.arange(1, across + 1, dtype=jnp.float32)
            hit = jnp.sum(table.astype(jnp.float32) * spot, axis=1).astype(jnp.int32) - 1
            target = hit[:, None] * rank + jnp.arange(rank, dtype=jnp.int32)
            target = jnp.where(hit[:, None] < 0, -1, target).reshape(down * rank)
            spots = jnp.arange(across * rank, dtype=jnp.int32)
            return (target[:, None] == spots[None, :]).astype(jnp.bfloat16)

        keep_wide = widen(keep)

        def stored(came):
            rows_of = lax.dot_general(
                keep_wide, came, (((0,), (0,)), ((), ())), preferred_element_type=jnp.float32
            )
            return rows_of.reshape(holder_count, rank, came.shape[1])

        alive = (slot_ids < group_live_counts[0]).astype(jnp.float32)
        alive = jnp.broadcast_to(alive[:, None], (slot_count, 128))
        key_value, grad_in, down_part, up_part = line_call(
            tensor_total,
            group_total,
            slot_count,
            activations.reshape(rows, dim_shard),
            frozen_weight,
            cotangent.reshape(rows, output_portion),
            alive,
            adapter_down_weight.reshape(holder_count * rank, dim_shard),
            adapter_up_weight.reshape(holder_count * rank, output_portion),
            keep_wide,
            widen(pick),
        )
        return (
            key_value.reshape(slot_count, seq_length, output_portion),
            grad_in.reshape(slot_count, seq_length, dim_shard),
            stored(down_part),
            stored(up_part),
        )
    every_down, every_up = (
        lax.all_gather(adapter_down_weight, "dp", axis=0, tiled=True),
        lax.all_gather(adapter_up_weight, "dp", axis=0, tiled=True),
    )
    mine_rows = lax.dynamic_slice_in_dim(adapter_rows, group_index * slot_count, slot_count)
    one_hot = (
        mine_rows[:, None] == jnp.arange(group_total * holder_count, dtype=jnp.int32)[None, :]
    ).astype(jnp.bfloat16)
    down_weight_slice = jnp.einsum(
        "ja,ard->jrd", one_hot, every_down, preferred_element_type=jnp.float32
    ).astype(jnp.bfloat16)
    up_weight_slice = jnp.einsum(
        "ja,arw->jrw", one_hot, every_up, preferred_element_type=jnp.float32
    ).astype(jnp.bfloat16)
    low_sum = lax.psum(
        jnp.einsum(
            "cfy,cjy->cfj", activations, down_weight_slice, preferred_element_type=jnp.float32
        ).astype(jnp.bfloat16),
        "tensor",
    )
    partial_value = jnp.dot(
        activations.reshape(slot_count * seq_length, dim_shard),
        frozen_weight,
        preferred_element_type=jnp.float32,
    ).reshape(slot_count, seq_length, full_out)
    whole_sum = lax.psum(partial_value.astype(jnp.bfloat16), "tensor").astype(jnp.float32)
    frozen_output = lax.dynamic_slice_in_dim(
        whole_sum, tensor_index * output_portion, output_portion, 2
    )
    live_mask_float = live_sequence_mask.astype(jnp.float32)
    adapter_contribution = jnp.einsum(
        "slr,srw->slw", low_sum, up_weight_slice, preferred_element_type=jnp.float32
    )
    key_value_output = (
        (frozen_output + adapter_scale * adapter_contribution) * live_mask_float
    ).astype(jnp.bfloat16)
    masked = cotangent * live_sequence_mask
    masked_full = lax.all_gather(masked, "tensor", axis=2, tiled=True)
    back_sum = lax.psum(
        (
            adapter_scale
            * jnp.einsum(
                "bvg,bqg->bvq", masked, up_weight_slice, preferred_element_type=jnp.float32
            )
        ).astype(jnp.bfloat16),
        "tensor",
    )
    frozen_path = lax.dot_general(
        masked_full.reshape(slot_count * seq_length, full_out),
        frozen_weight,
        (((1,), (1,)), ((), ())),
        preferred_element_type=jnp.float32,
    )
    input_gradient = frozen_path.reshape(slot_count, seq_length, dim_shard) + jnp.einsum(
        "qip,qpb->qib", back_sum, down_weight_slice, preferred_element_type=jnp.float32
    )
    grad_input = (input_gradient * live_mask_float).astype(jnp.bfloat16)
    down_contributions = jnp.einsum(
        "ihn,ihx->inx", back_sum, activations, preferred_element_type=jnp.float32
    )
    up_contributions = adapter_scale * jnp.einsum(
        "tun,tuq->tnq", low_sum, masked, preferred_element_type=jnp.float32
    )
    send_grad_down = jnp.einsum(
        "joc,jrd->ocrd", pick_table, down_contributions, precision=lax.Precision.HIGHEST
    )
    send_grad_up = jnp.einsum(
        "joc,jrw->ocrw", pick_table, up_contributions, precision=lax.Precision.HIGHEST
    )
    back_down, back_up = (
        lax.all_to_all(
            send_grad_down.astype(jnp.bfloat16), "dp", split_axis=0, concat_axis=0, tiled=True
        ).astype(send_grad_down.dtype),
        lax.all_to_all(
            send_grad_up.astype(jnp.bfloat16), "dp", split_axis=0, concat_axis=0, tiled=True
        ).astype(send_grad_up.dtype),
    )
    grad_down = jnp.einsum("eck,ecrd->krd", selection, back_down, precision=lax.Precision.HIGHEST)
    grad_up = jnp.einsum("eck,ecrw->krw", selection, back_up, precision=lax.Precision.HIGHEST)
    return (key_value_output, grad_input, grad_down, grad_up)


def solution(mesh):
    in_specs = (
        P(("parts", "dp"), None, "tensor"),
        P("tensor", None),
        P(("parts", "dp"), None, "tensor"),
        P(("parts", "dp"), None, "tensor"),
        P(("parts", "dp"), None, "tensor"),
        P("parts"),
        P("parts"),
        P(("parts", "dp")),
    )
    out_specs = (
        P(("parts", "dp"), None, "tensor"),
        P(("parts", "dp"), None, "tensor"),
        P(("parts", "dp"), None, "tensor"),
        P(("parts", "dp"), None, "tensor"),
    )
    return jax.shard_map(shards, mesh=mesh, in_specs=in_specs, out_specs=out_specs, check_vma=False)
```
